256 devices in a mesh: row: 8 (over x_lo, y), col: 32 (over z, x_hi, core).
Axes of the slice: x: 4 (x_hi: 2, x_lo: 2; x = x_hi * 2 + x_lo), y: 4, z: 8, core: 2. Of those that a mesh axis runs over, the one named last changes fastest.
Arguments:
- noise: float32 [4096, 4096], P('row', 'col'), may hold values from -20 to 20
- data: float32 [16384, 4096], P('col', 'row'), may hold values from -20 to 20
Outputs:
- noise_target: float32 [4096, 4096], P(('row', 'col'))
- data_target: float32 [16384, 4096], P('col', 'row')
The draws below stay inside these ranges and needn't reach their ends.
All inputs are finite; a program needn't handle non-finite values.
Results may differ from the reference program's by a relative error of at most 0.012.
The reference program's roundings to bfloat16 on the way (of `coupling`) count: a program that leaves them out, or rounds other values in their place, can miss the bound.
Values may be sent and summed in bfloat16 or wider, within the bound.
A program may use at most 64 MiB of HBM per device.

```python
import math
import jax
import jax.numpy as jnp

D = 4096
ITERS = 3
N = 4096
M = 16384


def latent_noise(key, ceiling):
    key = jax.random.fold_in(key, 11)
    k_normal = jax.random.fold_in(key, 0)
    k_scale = jax.random.fold_in(key, 2)
    gauss = jnp.clip(jax.random.normal(k_normal, (N, D), jnp.float32), -5.0, 5.0)
    values = gauss
    scales = jnp.exp(jax.random.uniform(k_scale, (N, 1), jnp.float32) * math.log(ceiling))
    planted = jnp.arange(16) * (N // 16)
    scales = scales.at[planted].set(ceiling)
    return jnp.clip(values * scales, -20.0, 20.0)


def draw_noise(key, part):
    return latent_noise(key, 10.0)


def draw_data(key, part):
    own_key = jax.random.fold_in(key, 5)
    k_normal = jax.random.fold_in(own_key, 0)
    k_scale = jax.random.fold_in(own_key, 2)
    ceiling = 10.0
    gauss = jnp.clip(jax.random.normal(k_normal, (M, D), jnp.float32), -5.0, 5.0)
    values = gauss
    scales = jnp.exp(jax.random.uniform(k_scale, (M, 1), jnp.float32) * math.log(ceiling))
    planted = jnp.arange(16) * (M // 16) + 2
    scales = scales.at[planted].set(ceiling)
    latents = values * scales
    return jnp.clip(latents, -20.0, 20.0)


def setup_inputs(seed: int = 0) -> dict:
    key_of = jax.random.split(jax.random.key(seed), 3)
    noise = draw_noise(jax.random.fold_in(key_of[2], 71), 0)
    data = draw_data(jax.random.fold_in(key_of[2], 71), 0)
    return dict(noise=noise, data=data)


entropy_weight = 0.25


def reference(noise, data):
    noise_half = noise.astype(jnp.bfloat16)
    data_half = data.astype(jnp.bfloat16)
    noise_square = jnp.sum(jnp.square(noise_half.astype(jnp.float32)), axis=1)
    data_square = jnp.sum(jnp.square(data_half.astype(jnp.float32)), axis=1)
    products = jnp.dot(noise_half, data_half.T, preferred_element_type=jnp.float32)
    distance = (noise_square[:, None] + data_square[None, :] - 2.0 * products) / D
    log_rows = math.log(N)
    log_cols = math.log(M)
    pot_data = jnp.zeros((M,), jnp.float32)
    pot_noise = jnp.zeros((N,), jnp.float32)
    for iteration in range(ITERS):
        scores = (pot_data[None, :] - distance) / entropy_weight
        pot_noise = -entropy_weight * (jax.nn.logsumexp(scores, axis=1) + log_rows)
        scores = (pot_noise[:, None] - distance) / entropy_weight
        pot_data = -entropy_weight * (jax.nn.logsumexp(scores, axis=0) + log_cols)
    coupling = jnp.exp((pot_noise[:, None] + pot_data[None, :] - distance) / entropy_weight + log_rows + log_cols).astype(jnp.bfloat16)
    row_mass = jnp.sum(coupling.astype(jnp.float32), axis=1)
    col_mass = jnp.sum(coupling.astype(jnp.float32), axis=0)
    noise_target = jnp.dot(coupling, data_half, preferred_element_type=jnp.float32) / row_mass[:, None]
    data_target = jnp.dot(coupling.T, noise_half, preferred_element_type=jnp.float32) / col_mass[:, None]
    return noise_target, data_target
```

```python
import functools
import math

import jax
import jax.numpy as jnp
from jax import lax
from jax.experimental import pallas as pl
from jax.experimental.pallas import tpu as pltpu
from jax.sharding import PartitionSpec as P

ITERS = 3
YN = 4
ROWS = 8
MESH = pl.DeviceIdType.MESH
F32 = jnp.float32
BF16 = jnp.bfloat16
NT = (((1,), (1,)), ((), ()))
NN = (((1,), (0,)), ((), ()))


def remote(src, dst, send, recv, **dev):
    return pltpu.make_async_remote_copy(
        src_ref=src, dst_ref=dst, send_sem=send, recv_sem=recv,
        device_id=dev, device_id_type=MESH,
    )


def landed(ref, sem):
    pltpu.make_async_copy(ref, ref, sem).wait()


def column(rows4):
    blocks = [
        jnp.transpose(jnp.broadcast_to(rows4[k:k + 1, :], (128, 128)))
        for k in range(rows4.shape[0])
    ]
    return jnp.concatenate(blocks, axis=0)


def local_lse(mat, col, out):
    q = mat.shape[1] // 128
    for k in range(q):
        x = col[...] - mat[:, k * 128:(k + 1) * 128]
        m = jnp.max(x, axis=0, keepdims=True)
        s = jnp.sum(jnp.exp2(x - m), axis=0, keepdims=True)
        out[k:k + 1, :] = m
        out[q + k:q + k + 1, :] = s


def combine(parts):
    q = parts.shape[1] // 2
    m = parts[:, :q, :]
    s = parts[:, q:, :]
    top = jnp.max(m, axis=0)
    return top, jnp.sum(s * jnp.exp2(m - top[None]), axis=0)


def kernel(
    cfg, noise_ref, data_ref, nt_ref, dt_ref,
    noise_f, data_f, s_nm, s_mn, c_nm, c_mn, u_col, v_col, sq_n, sq_m, u_row, v_row,
    core_x, col_x, row_x,
    p_b, rb3, rb_half, rb4, rb5, q_b, q_r, q_s, z_first, z_next, h_out, h_in, own,
    nsend, nrecv, dsend, drecv,
    core_send, core_recv, col_send, col_recv, row_send, row_recv,
    psend, precv, qsend, qrecv, zsend, zrecv,
):
    zn, stage = cfg
    nb = noise_ref.shape[0]
    mb = data_ref.shape[0]
    kd = data_ref.shape[1]
    kn = noise_ref.shape[1]
    cols = 4 * zn
    npp = cols // ROWS
    zh_n = 2 * zn
    half = mb // 2
    features = kd * ROWS
    scale = math.log2(math.e) / (0.25 * features)
    log_rows = math.log2(nb * ROWS)
    log_cols = math.log2(mb * cols)

    row = lax.axis_index("row")
    col = lax.axis_index("col")
    xl = lax.div(row, YN)
    y = lax.rem(row, YN)
    z = lax.div(col, 4)
    h = lax.rem(lax.div(col, 2), 2)
    c = lax.rem(col, 2)

    def rid(dx, dy):
        return lax.rem(xl + dx, 2) * YN + lax.rem(y + dy, YN)

    def zz(d):
        return lax.rem(z + d + zn, zn)

    def cid(zi, hi, ci):
        return (zi * 2 + hi) * 2 + ci

    y_up, y_dn, x_p = rid(0, 1), rid(0, 3), rid(1, 0)
    z_up, z_dn = cid(zz(1), h, c), cid(zz(-1), h, c)
    h_p = cid(z, 1 - h, c)
    c_p = cid(z, h, 1 - c)
    zh = z * 2 + h

    noise_f[col] = noise_ref[...].astype(BF16)
    data_f[row] = data_ref[...].astype(BF16)

    barrier = pltpu.get_barrier_semaphore()

    def greet(**dev):
        pl.semaphore_signal(barrier, inc=1, device_id=dev, device_id_type=MESH)

    for d in range(1, ROWS):
        greet(row=lax.rem(row + d, ROWS))
    greet(col=c_p)
    for d in range(1, zh_n):
        greet(col=lax.rem(zh + d, zh_n) * 2 + c)
    pl.semaphore_wait(barrier, ROWS - 1 + 1 + zh_n - 1)

    pending = []
    n_count = [0]
    d_count = [0]

    def send_noise(piece, dev):
        k = n_count[0]
        n_count[0] += 1
        cp = remote(noise_f.at[piece], noise_f.at[piece], nsend.at[k], nrecv.at[piece], col=dev)
        cp.start()
        pending.append(cp)

    def got_noise(piece):
        landed(noise_f.at[piece], nrecv.at[piece])

    def data_half(r, i):
        return data_f.at[r, pl.ds(i * half, half), :]

    def send_data(r, i, dev):
        k = d_count[0]
        d_count[0] += 1
        cp = remote(data_half(r, i), data_half(r, i), dsend.at[k], drecv.at[r, i], row=dev)
        cp.start()
        pending.append(cp)

    def got_data(r, i):
        landed(data_half(r, i), drecv.at[r, i])

    send_noise(col, z_up)
    send_noise(col, z_dn)
    send_noise(col, h_p)
    send_noise(col, c_p)
    for i in (0, 1):
        send_data(row, i, y_up)
        send_data(row, 1 - i, y_dn)
        send_data(row, i, x_p)

    zhalf = zn // 2

    def noise_step(s):
        if s < zhalf:
            for hi in (h, 1 - h):
                up, dn = cid(zz(-s), hi, c), cid(zz(s), hi, c)
                got_noise(up)
                if s < zhalf - 1:
                    send_noise(up, z_up)
                send_noise(up, c_p)
                got_noise(dn)
                if s < zhalf - 1:
                    send_noise(dn, z_dn)
                send_noise(dn, c_p)
            if s == zhalf - 1:
                send_noise(cid(zz(-s), 0, c), z_up)
                send_noise(cid(zz(s), 1, c), z_dn)
        else:
            far = zz(zhalf)
            for hi in (0, 1):
                got_noise(cid(far, hi, c))
                send_noise(cid(far, hi, c), c_p)

    got_noise(h_p)
    if zhalf > 1:
        send_noise(h_p, z_up)
        send_noise(h_p, z_dn)
    else:
        raise NotImplementedError
    send_noise(h_p, c_p)
    noise_step(1)
    got_data(y_dn, 0)
    send_data(y_dn, 0, y_up)
    got_data(y_up, 1)
    send_data(y_up, 1, y_dn)
    got_data(x_p, 0)
    send_data(x_p, 0, y_up)
    send_data(x_p, 0, y_dn)
    if zhalf > 2:
        noise_step(2)
    got_data(x_p, 1)
    send_data(x_p, 1, y_up)
    send_data(x_p, 1, y_dn)
    for i in (0, 1):
        got_data(rid(0, 2), i)
        send_data(rid(0, 2), i, x_p)
    for s in range(3, zhalf + 1):
        noise_step(s)
    if zhalf == 2:
        noise_step(2)
    for zi in range(zn):
        for hi in (0, 1):
            got_noise(cid(zi, hi, 1 - c))
    got_data(y_dn, 1)
    got_data(y_up, 0)

    s_nm[...] = jnp.zeros_like(s_nm)
    s_mn[...] = jnp.zeros_like(s_mn)
    sq_n[...] = jnp.zeros_like(sq_n)
    sq_m[...] = jnp.zeros_like(sq_m)

    def noise_cat(r):
        return jnp.concatenate([noise_f[r * npp + i] for i in range(npp)], axis=1)

    def chunk(r):
        a = noise_cat(r)
        d = data_f[r]
        s_nm[...] += lax.dot_general(a, d, NT, preferred_element_type=F32)
        s_mn[...] += lax.dot_general(d, a, NT, preferred_element_type=F32)
        for sq, v in ((sq_n, a), (sq_m, d)):
            total = sq[...]
            for i in range(v.shape[1] // 128):
                w = v[:, i * 128:(i + 1) * 128].astype(F32)
                total += w * w
            sq[...] = total

    def first(k, carry):
        dx = jnp.where(k == 3, 1, 0)
        dy = jnp.where(k == 1, 1, jnp.where(k == 2, 3, jnp.where(k == 4, 2, 0)))
        chunk(rid(dx, dy))
        return carry

    lax.fori_loop(0, 5, first, 0)

    def last(k, carry):
        dy = jnp.where(k == 0, 1, jnp.where(k == 1, 3, 2))
        r = rid(1, dy)
        got_data(r, 0)
        got_data(r, 1)
        chunk(r)
        return carry

    lax.fori_loop(0, 3, last, 0)

    def rows_of(sq):
        t = jnp.sum(jnp.transpose(sq), axis=0, keepdims=True)
        return jnp.concatenate([t[:, k * 128:(k + 1) * 128] for k in range(t.shape[1] // 128)], axis=0)

    ns = rows_of(sq_n[...])
    ds = rows_of(sq_m[...])
    u_col[...] = column(ns)
    v_col[...] = column(ds)
    for k in range(mb // 128):
        at = (slice(None), slice(k * 128, (k + 1) * 128))
        s_nm[at] = (u_col[...] + ds[k:k + 1, :] - 2.0 * s_nm[at]) * scale
    for k in range(nb // 128):
        at = (slice(None), slice(k * 128, (k + 1) * 128))
        s_mn[at] = (v_col[...] + ns[k:k + 1, :] - 2.0 * s_mn[at]) * scale

    def start_core(t):
        cp = remote(core_x.at[t, c], core_x.at[t, c], core_send.at[t], core_recv.at[t], col=c_p)
        cp.start()
        pending.append(cp)

    def start_col(t):
        for d in range(1, zh_n):
            remote(col_x.at[t, zh], col_x.at[t, zh], col_send.at[t], col_recv.at[t],
                   col=lax.rem(zh + d, zh_n) * 2 + c).start()

    def start_row(t):
        for d in range(1, ROWS):
            remote(row_x.at[t, row], row_x.at[t, row], row_send.at[t], row_recv.at[t],
                   row=lax.rem(row + d, ROWS)).start()

    def got_col(t):
        landed(col_x.at[t, pl.ds(0, zh_n - 1)], col_recv.at[t])

    def got_row(t):
        landed(row_x.at[t, pl.ds(0, ROWS - 1)], row_recv.at[t])

    if stage >= 2:
        v_col[...] = jnp.zeros_like(v_col)
        qn, qm = nb // 128, mb // 128
        for t in range(ITERS):
            local_lse(s_mn, v_col, core_x.at[t, c])
            start_core(t)
            landed(core_x.at[t, 1 - c], core_recv.at[t])
            top, total = combine(core_x[t])
            col_x[t, zh, 0:qn, :] = top
            col_x[t, zh, qn:2 * qn, :] = total
            start_col(t)
            got_col(t)
            top, total = combine(col_x[t])
            u = -(top + jnp.log2(total) + log_rows)
            u_row[...] = u
            u_col[...] = column(u)
            local_lse(s_nm, u_col, row_x.at[t, row])
            start_row(t)
            got_row(t)
            top, total = combine(row_x[t])
            v = -(top + jnp.log2(total) + log_cols)
            v_row[...] = v
            v_col[...] = column(v)

    if stage >= 3:
        t = ITERS
        logs = log_rows + log_cols
        core_x[t, c] = jnp.zeros(core_x.shape[2:], F32)
        row_x[t, row] = jnp.zeros(row_x.shape[2:], F32)
        for k in range(nb // 128):
            at = (slice(None), slice(k * 128, (k + 1) * 128))
            w = jnp.exp2(v_col[...] + u_row[k:k + 1, :] - s_mn[at] + logs).astype(BF16)
            c_mn[at] = w
            core_x[t, c, k:k + 1, :] = jnp.sum(w.astype(F32), axis=0, keepdims=True)
        start_core(t)

        def p_dot(r):
            return lax.dot_general(c_mn[...], noise_cat(r), NN, preferred_element_type=F32)

        def lead(k, carry):
            r = rid(1, jnp.where(k == 0, 2, jnp.where(k == 1, 1, 3)))
            dev = jnp.where(k == 0, x_p, jnp.where(k == 1, y_up, y_dn))
            p_b[r] = p_dot(r).astype(BF16)
            remote(p_b.at[r], rb3.at[k], psend.at[k], precv.at[k], row=dev).start()
            return carry

        lax.fori_loop(0, 3, lead, 0)

        for k in range(mb // 128):
            at = (slice(None), slice(k * 128, (k + 1) * 128))
            w = jnp.exp2(u_col[...] + v_row[k:k + 1, :] - s_nm[at] + logs).astype(BF16)
            c_nm[at] = w
            row_x[t, row, k:k + 1, :] = jnp.sum(w.astype(F32), axis=0, keepdims=True)
        start_row(t)

        def lanes(r):
            return pl.ds(pl.multiple_of(r * kd, kd), kd)

        share = nb // cols

        def q_loop(r, carry):
            w = lax.dot_general(c_nm[...], data_f[r], NN, preferred_element_type=F32)
            q_b[:, :, :, lanes(r)] = w.astype(BF16).reshape(zh_n, 2, share, kd)
            remote(q_b.at[:, 1 - c, :, lanes(r)], q_r.at[:, :, lanes(r)],
                   qsend.at[r], qrecv.at[r], col=c_p).start()
            return carry

        lax.fori_loop(0, ROWS, q_loop, 0)

        def q_sum(r, carry):
            landed(q_r.at[:, :, lanes(r)], qrecv.at[r])
            q_s[:, :, lanes(r)] = (
                q_b[:, c, :, lanes(r)].astype(F32) + q_r[:, :, lanes(r)].astype(F32)
            ).astype(BF16)
            return carry

        lax.fori_loop(0, ROWS, q_sum, 0)

        landed(core_x.at[t, 1 - c], core_recv.at[t])
        col_x[t, zh] = core_x[t, 0] + core_x[t, 1]
        start_col(t)

        z_count = [0]

        def z_send(src, dst, sem, dev):
            k = z_count[0]
            z_count[0] += 1
            cp = remote(src, dst, zsend.at[k], zrecv.at[sem], col=dev)
            cp.start()
            pending.append(cp)

        far = zz(zhalf)
        z_send(q_s.at[far * 2], z_first.at[0], 0, z_up)
        z_send(q_s.at[far * 2 + 1], z_first.at[1], 1, z_dn)

        def rest(k, carry):
            dx = jnp.where(k == 1, 1, 0)
            dy = jnp.where(k == 0, 2, jnp.where(k == 2, 1, jnp.where(k == 3, 3, 0)))
            r = rid(dx, dy)
            p_b[r] = p_dot(r).astype(BF16)
            return carry

        lax.fori_loop(0, 5, rest, 0)

        def z_step(s):
            for i, sign, dev in ((0, 1, z_up), (1, -1, z_dn)):
                dest = zz(sign * (zhalf - s))
                if s == 1:
                    landed(z_first.at[i], zrecv.at[i])
                    q_s[dest * 2 + i] = (q_s[dest * 2 + i].astype(F32) + z_first[i].astype(F32)).astype(BF16)
                else:
                    landed(z_next.at[s - 2, i], zrecv.at[2 * (s - 1) + i])
                    two = pl.ds(dest * 2, 2)
                    q_s[two] = (q_s[two].astype(F32) + z_next[s - 2, i].astype(F32)).astype(BF16)
                z_send(q_s.at[pl.ds(dest * 2, 2)], z_next.at[s - 1, i], 2 * s + i, dev)

        z_step(1)

        def add_to(r, i, ref):
            at = pl.ds(i * half, half)
            p_b[r, at, :] = (p_b[r, at, :].astype(F32) + ref.astype(F32)).astype(BF16)

        def p_send(k, src, dst, dev):
            cp = remote(src, dst, psend.at[k], precv.at[k], row=dev)
            cp.start()
            pending.append(cp)

        landed(rb3.at[0], precv.at[0])
        r2 = rid(0, 2)
        add_to(r2, 0, rb3[0, :half])
        p_send(3, p_b.at[r2, pl.ds(0, half), :], rb_half.at[0], y_up)
        add_to(r2, 1, rb3[0, half:])
        p_send(4, p_b.at[r2, pl.ds(half, half), :], rb_half.at[1], y_dn)
        landed(rb3.at[1], precv.at[1])
        landed(rb3.at[2], precv.at[2])
        p_b[x_p] = (p_b[x_p].astype(F32) + rb3[1].astype(F32) + rb3[2].astype(F32)).astype(BF16)
        p_send(5, p_b.at[x_p], rb4, x_p)
        if zhalf > 2:
            z_step(2)
        landed(rb_half.at[0], precv.at[3])
        add_to(y_up, 0, rb_half[0])
        p_send(6, p_b.at[y_up], rb5.at[0], y_up)
        landed(rb_half.at[1], precv.at[4])
        add_to(y_dn, 1, rb_half[1])
        p_send(7, p_b.at[y_dn], rb5.at[1], y_dn)
        for s in range(3, zhalf):
            z_step(s)

        for i in (0, 1):
            landed(z_next.at[zhalf - 2, i], zrecv.at[2 * (zhalf - 1) + i])
        mine = q_s[pl.ds(z * 2, 2)].astype(F32) + z_next[zhalf - 2, 0].astype(F32) + z_next[zhalf - 2, 1].astype(F32)
        own[...] = mine
        h_out[...] = own[1 - h].astype(BF16)
        z_send(h_out, h_in, 2 * zhalf, h_p)

        got_row(t)
        qm = mb // 128
        col_mass = jnp.sum(row_x[t], axis=0)[:qm]
        v_col[...] = column(1.0 / col_mass)
        got_col(t)
        qn = nb // 128
        row_mass = jnp.sum(col_x[t], axis=0)[:qn]
        u_col[...] = column(1.0 / row_mass)

        landed(rb4, precv.at[5])
        landed(rb5.at[0], precv.at[6])
        landed(rb5.at[1], precv.at[7])
        for k in range(kd // 128):
            at = slice(k * 128, (k + 1) * 128)
            dt_ref[:, at] = v_col[...] * (
                p_b[row, :, at].astype(F32) + rb4[:, at].astype(F32)
                + rb5[0, :, at].astype(F32) + rb5[1, :, at].astype(F32)
            )
        landed(h_in, zrecv.at[2 * zhalf])
        inv = u_col[pl.ds(pl.multiple_of(col * share, share), share), :]
        for k in range(nt_ref.shape[1] // 128):
            at = slice(k * 128, (k + 1) * 128)
            nt_ref[:, at] = inv * (own[h, :, at] + h_in[:, at].astype(F32))

    for cp in pending:
        cp.wait_send()
    for t in range(ITERS + 1):
        if (stage >= 2 and t < ITERS) or stage >= 3:
            landed(col_x.at[t, pl.ds(0, zh_n - 1)], col_send.at[t])
            landed(row_x.at[t, pl.ds(0, ROWS - 1)], row_send.at[t])
    if stage >= 3:
        for k in range(3):
            landed(rb3.at[k], psend.at[k])

        def left(r, carry):
            landed(q_r.at[:, :, lanes(r)], qsend.at[r])
            return carry

        lax.fori_loop(0, ROWS, left, 0)
    if stage < 3:
        nt_ref[...] = jnp.zeros_like(nt_ref)
        dt_ref[...] = s_nm[...] + s_mn[...]


def local(noise, data, zn, stage=3):
    nb, kn = noise.shape
    mb, kd = data.shape
    cols = 4 * zn
    zh_n = 2 * zn
    features = kd * ROWS
    share = nb // cols
    half = mb // 2
    zhalf = zn // 2
    vm = pltpu.VMEM
    dma = pltpu.SemaphoreType.DMA
    ex = ITERS + 1
    scratch = [
        vm((cols, nb, kn), BF16), vm((ROWS, mb, kd), BF16),
        vm((nb, mb), F32), vm((mb, nb), F32), vm((nb, mb), BF16), vm((mb, nb), BF16),
        vm((nb, 128), F32), vm((mb, 128), F32), vm((nb, 128), F32), vm((mb, 128), F32),
        vm((nb // 128, 128), F32), vm((mb // 128, 128), F32),
        vm((ex, 2, nb // 64, 128), F32), vm((ex, zh_n, nb // 64, 128), F32), vm((ex, ROWS, mb // 64, 128), F32),
        vm((ROWS, mb, kd), BF16), vm((3, mb, kd), BF16), vm((2, half, kd), BF16),
        vm((mb, kd), BF16), vm((2, mb, kd), BF16),
        vm((zh_n, 2, share, features), BF16), vm((zh_n, share, features), BF16), vm((zh_n, share, features), BF16),
        vm((2, share, features), BF16), vm((zhalf - 1, 2, 2, share, features), BF16),
        vm((share, features), BF16), vm((share, features), BF16), vm((2, share, features), F32),
        dma((40,)), dma((cols,)), dma((16,)), dma((ROWS, 2)),
        dma((ex,)), dma((ex,)), dma((ex,)), dma((ex,)), dma((ex,)), dma((ex,)),
        dma((8,)), dma((8,)), dma((ROWS,)), dma((ROWS,)), dma((2 * zhalf + 1,)), dma((2 * zhalf + 1,)),
    ]
    return pl.pallas_call(
        functools.partial(kernel, (zn, stage)),
        out_shape=(
            jax.ShapeDtypeStruct((share, features), F32),
            jax.ShapeDtypeStruct((mb, kd), F32),
        ),
        in_specs=[pl.BlockSpec(memory_space=pltpu.VMEM)] * 2,
        out_specs=[pl.BlockSpec(memory_space=pltpu.VMEM)] * 2,
        scratch_shapes=scratch,
        compiler_params=pltpu.CompilerParams(
            collective_id=0, has_side_effects=True, vmem_limit_bytes=56 * 1024 * 1024
        ),
    )(noise, data)


def solution(mesh, stage=3):
    zn = mesh.shape["col"] // 4
    return jax.shard_map(
        functools.partial(local, zn=zn, stage=stage),
        mesh=mesh,
        in_specs=(P("row", "col"), P("col", "row")),
        out_specs=(P(("row", "col"), None), P("col", "row")),
        check_vma=False,
    )
```

```python
import functools
import math

import jax
import jax.numpy as jnp
from jax import lax
from jax.experimental import pallas as pl
from jax.experimental.pallas import tpu as pltpu
from jax.sharding import PartitionSpec as P

ITERS = 3
YN = 4
ROWS = 8
ZN = 8
PARTS = 4
MESH = pl.DeviceIdType.MESH
F32 = jnp.float32
BF16 = jnp.bfloat16
NT = (((1,), (1,)), ((), ()))
NN = (((1,), (0,)), ((), ()))


def remote(src, dst, send, recv, **dev):
    return pltpu.make_async_remote_copy(
        src_ref=src, dst_ref=dst, send_sem=send, recv_sem=recv,
        device_id=dev, device_id_type=MESH,
    )


def landed(ref, sem):
    pltpu.make_async_copy(ref, ref, sem).wait()


def column(rows4):
    blocks = [
        jnp.transpose(jnp.broadcast_to(rows4[k:k + 1, :], (128, 128)))
        for k in range(rows4.shape[0])
    ]
    return jnp.concatenate(blocks, axis=0)


def local_lse(mat, col, out):
    for k in range(mat.shape[1] // 128):
        x = col[...] - mat[:, k * 128:(k + 1) * 128]
        m = jnp.max(x, axis=0, keepdims=True)
        s = jnp.sum(jnp.exp2(x - m), axis=0, keepdims=True)
        out[k:k + 1, :] = m + jnp.log2(s)


def combine(parts):
    top = jnp.max(parts, axis=0)
    return top + jnp.log2(jnp.sum(jnp.exp2(parts - top[None]), axis=0))


def kernel(
    cfg, noise_ref, data_ref, nt_ref, dt_ref,
    noise_f, data_f, s_nm, s_mn, c_nm, c_mn, u_col, v_col, sq_n, sq_m, u_row, v_row,
    core_x, col_x, row_x,
    p_b, p_lead, p_half, p_x, p_next, q_b, q_r, q_s, z_first, z_next, h_out, h_in, own,
    nsend, nrecv, dsend, drecv,
    core_send, core_recv, col_send, col_recv, row_send, row_recv,
    psend, precv, p2send, p2recv, qsend, qrecv, zsend, zrecv, hrecv,
):
    stage, opts = cfg
    zn = ZN
    nb = noise_ref.shape[0]
    mb = data_ref.shape[0]
    kd = data_ref.shape[1]
    kn = noise_ref.shape[1]
    cols = 4 * zn
    npp = cols // ROWS
    zh_n = 2 * zn
    half = mb // 2
    part = mb // PARTS
    fold = nb // 2
    features = kd * ROWS
    scale = math.log2(math.e) / (0.25 * features)
    log_rows = math.log2(nb * ROWS)
    log_cols = math.log2(mb * cols)

    row = lax.axis_index("row")
    col = lax.axis_index("col")
    xl = lax.div(row, YN)
    y = lax.rem(row, YN)
    z = lax.div(col, 4)
    h = lax.rem(lax.div(col, 2), 2)
    c = lax.rem(col, 2)

    def rid(dx, dy):
        return lax.rem(xl + dx, 2) * YN + lax.rem(y + dy, YN)

    def zz(d):
        return lax.rem(z + d + zn, zn)

    def cid(zi, hi, ci):
        return (zi * 2 + hi) * 2 + ci

    y_up, y_dn, x_p = rid(0, 1), rid(0, 3), rid(1, 0)
    z_up, z_dn = cid(zz(1), h, c), cid(zz(-1), h, c)
    h_p = cid(z, 1 - h, c)
    c_p = cid(z, h, 1 - c)
    zh = z * 2 + h

    noise_f[col] = noise_ref[...].astype(BF16)
    data_f[row] = data_ref[...].astype(BF16)

    barrier = pltpu.get_barrier_semaphore()

    def greet(**dev):
        pl.semaphore_signal(barrier, inc=1, device_id=dev, device_id_type=MESH)

    for dev in (y_up, y_dn, x_p):
        greet(row=dev)
    for dev in (z_up, z_dn, h_p, c_p):
        greet(col=dev)
    pl.semaphore_wait(barrier, 7)

    pending = []
    n_count = [0]
    d_count = [0]

    def noise_part(piece, i):
        return noise_f.at[piece, pl.ds(i * fold, fold), :]

    def send_noise(piece, i, dev):
        k = n_count[0]
        n_count[0] += 1
        ref = noise_f.at[piece] if i is None else noise_part(piece, i)
        cp = remote(ref, ref, nsend.at[k], nrecv.at[piece, 0 if i is None else i], col=dev)
        cp.start()
        pending.append(cp)

    def got_noise(piece, i):
        ref = noise_f.at[piece] if i is None else noise_part(piece, i)
        landed(ref, nrecv.at[piece, 0 if i is None else i])

    def data_part(r, i):
        return data_f.at[r, pl.ds(i * part, part), :]

    def send_data(r, i, dev):
        k = d_count[0]
        d_count[0] += 1
        cp = remote(data_part(r, i), data_part(r, i), dsend.at[k], drecv.at[r, i], row=dev)
        cp.start()
        pending.append(cp)

    def got_data(r, i):
        landed(data_part(r, i), drecv.at[r, i])

    across = rid(0, 2)
    for i in (0, 1):
        send_noise(col, i, h_p)
        send_noise(col, i, z_up)
        send_noise(col, i, z_dn)
        send_data(row, i, y_up)
        send_data(row, i + 2, y_dn)
        send_data(row, i, x_p)
    send_data(row, 2, y_up)
    send_data(row, 0, y_dn)
    send_data(row, 2, x_p)
    send_data(row, 3, x_p)
    send_noise(col, None, c_p)

    def noise_got(s, hi, i):
        up, dn = cid(zz(-s), hi, c), cid(zz(s), hi, c)
        got_noise(up, i)
        if s < 3 or i == 0:
            send_noise(up, i, z_up)
        got_noise(dn, i)
        if s < 3 or i == 1:
            send_noise(dn, i, z_dn)
        if i == 1:
            send_noise(up, None, c_p)
            send_noise(dn, None, c_p)

    def noise_pair(i):
        got_noise(h_p, i)
        send_noise(h_p, i, z_up)
        send_noise(h_p, i, z_dn)
        if i == 1:
            send_noise(h_p, None, c_p)

    def pass_on(i):
        got_data(y_dn, i)
        send_data(y_dn, i, y_up)
        got_data(y_up, i + 2)
        send_data(y_up, i + 2, y_dn)

    def from_x(i):
        got_data(x_p, i)
        send_data(x_p, i, y_up)
        send_data(x_p, i, y_dn)

    def to_x(i):
        for k in (i, i + 2):
            got_data(across, k)
            send_data(across, k, x_p)

    g = 1 - h
    noise_got(1, h, 0)
    noise_pair(0)
    pass_on(0)
    noise_got(1, h, 1)
    noise_pair(1)
    noise_got(2, h, 0)
    pass_on(1)
    send_data(row, 3, y_up)
    send_data(row, 1, y_dn)
    from_x(0)
    noise_got(2, h, 1)
    noise_got(1, g, 0)
    from_x(1)
    noise_got(3, h, 0)
    noise_got(1, g, 1)
    noise_got(3, h, 1)
    from_x(2)
    to_x(0)
    noise_got(2, g, 0)
    from_x(3)
    to_x(1)
    noise_got(2, g, 1)
    noise_got(3, g, 0)
    noise_got(3, g, 1)
    for i in (2, 3):
        got_data(y_dn, i)
        got_data(y_up, i - 2)

    s_nm[...] = jnp.zeros_like(s_nm)
    s_mn[...] = jnp.zeros_like(s_mn)
    sq_n[...] = jnp.zeros_like(sq_n)
    sq_m[...] = jnp.zeros_like(sq_m)

    def noise_cat(r):
        return jnp.concatenate([noise_f[r * npp + i] for i in range(npp)], axis=1)

    def squares(sq, at, v):
        total = sq[at, :]
        for i in range(v.shape[1] // 128):
            w = v[:, i * 128:(i + 1) * 128].astype(F32)
            total += w * w
        sq[at, :] = total

    def chunk(r, k=None):
        at = pl.ds(0, mb) if k is None else pl.ds(k * half, half)
        a = noise_cat(r)
        d = data_f[r, at, :]
        s_nm[:, at] += lax.dot_general(a, d, NT, preferred_element_type=F32)
        s_mn[at, :] += lax.dot_general(d, a, NT, preferred_element_type=F32)
        squares(sq_m, at, d)
        if k != 1:
            squares(sq_n, pl.ds(0, nb), a)

    def plane(k):
        step = lax.div(k + 1, 2)
        zi = zz(jnp.where(lax.rem(k, 2) == 0, step, -step))
        for hi in (0, 1):
            got_noise(cid(zi, hi, 1 - c), None)

        @pl.when((lax.div(zi, YN) == xl) | (lax.rem(zi, YN) == y))
        def _():
            chunk(zi)

    def near_plane(k, carry):
        plane(k)
        return carry

    lax.fori_loop(0, 5, near_plane, 0)
    far = zz(4)
    for hi in (0, 1):
        for i in (0, 1):
            got_noise(cid(far, hi, c), i)
        send_noise(cid(far, hi, c), None, c_p)
    lax.fori_loop(5, 8, near_plane, 0)

    def sides(k):
        def body(j, carry):
            r = rid(1, jnp.where(j == 0, 1, 3))
            for i in (2 * k, 2 * k + 1):
                got_data(r, i)
            chunk(r, k)
            return carry

        lax.fori_loop(0, 2, body, 0)

    sides(0)
    for i in range(PARTS):
        got_data(rid(1, 2), i)
    chunk(rid(1, 2))
    sides(1)

    def rows_of(sq):
        t = jnp.sum(jnp.transpose(sq), axis=0, keepdims=True)
        return jnp.concatenate([t[:, k * 128:(k + 1) * 128] for k in range(t.shape[1] // 128)], axis=0)

    ns = rows_of(sq_n[...])
    ds = rows_of(sq_m[...])
    u_col[...] = column(ns)
    v_col[...] = column(ds)
    for k in range(mb // 128):
        at = (slice(None), slice(k * 128, (k + 1) * 128))
        s_nm[at] = (u_col[...] + ds[k:k + 1, :] - 2.0 * s_nm[at]) * scale
    for k in range(nb // 128):
        at = (slice(None), slice(k * 128, (k + 1) * 128))
        s_mn[at] = (v_col[...] + ns[k:k + 1, :] - 2.0 * s_mn[at]) * scale

    col_to = [cid(zz(d), hi, c) for d in (4, 3, -3, 2, -2, 1, -1, 0) for hi in (1 - h, h)][:-1]
    row_to = [rid(dx, dy) for dy in (2, 1, 3, 0) for dx in (1, 0)][:-1]

    def start_core(t):
        cp = remote(core_x.at[t, c], core_x.at[t, c], core_send.at[t], core_recv.at[t], col=c_p)
        cp.start()
        pending.append(cp)

    def start_col(t):
        for to in col_to:
            remote(col_x.at[t, zh], col_x.at[t, zh], col_send.at[t], col_recv.at[t], col=to).start()

    def start_row(t):
        for to in row_to:
            remote(row_x.at[t, row], row_x.at[t, row], row_send.at[t], row_recv.at[t], row=to).start()

    def got_col(t):
        landed(col_x.at[t, pl.ds(0, zh_n - 1)], col_recv.at[t])

    def got_row(t):
        landed(row_x.at[t, pl.ds(0, ROWS - 1)], row_recv.at[t])

    if stage >= 2:
        v_col[...] = jnp.zeros_like(v_col)
        for t in range(ITERS):
            local_lse(s_mn, v_col, core_x.at[t, c])
            start_core(t)
            landed(core_x.at[t, 1 - c], core_recv.at[t])
            col_x[t, zh] = combine(core_x[t])
            start_col(t)
            got_col(t)
            u = -(combine(col_x[t]) + log_rows)
            u_row[...] = u
            u_col[...] = column(u)
            local_lse(s_nm, u_col, row_x.at[t, row])
            start_row(t)
            got_row(t)
            v = -(combine(row_x[t]) + log_cols)
            v_row[...] = v
            v_col[...] = column(v)

    wide = features // 2

    def lanes(r):
        return pl.ds(pl.multiple_of(r * kd, kd), kd)

    if stage >= 3:
        t = ITERS
        logs = log_rows + log_cols
        for k in range(nb // 128):
            at = (slice(None), slice(k * 128, (k + 1) * 128))
            w = jnp.exp2(v_col[...] + u_row[k:k + 1, :] - s_mn[at] + logs).astype(BF16)
            c_mn[at] = w
            core_x[t, c, k:k + 1, :] = jnp.sum(w.astype(F32), axis=0, keepdims=True)
        start_core(t)

        def p_dot(r):
            p_b[r] = lax.dot_general(c_mn[...], noise_cat(r), NN, preferred_element_type=F32).astype(BF16)

        def p_half_of(r, i):
            return p_b.at[r, pl.ds(i * half, half), :]

        def lead(k, carry):
            r = rid(1, jnp.where(k == 0, 1, jnp.where(k == 1, 3, 2)))
            dev = jnp.where(k == 0, y_up, jnp.where(k == 1, y_dn, x_p))
            p_dot(r)
            for i in (0, 1):
                remote(p_half_of(r, i), p_lead.at[k, i], psend.at[k, i], precv.at[k, i], row=dev).start()
            return carry

        lax.fori_loop(0, 3, lead, 0)

        for k in range(mb // 128):
            at = (slice(None), slice(k * 128, (k + 1) * 128))
            w = jnp.exp2(u_col[...] + v_row[k:k + 1, :] - s_nm[at] + logs).astype(BF16)
            c_nm[at] = w
            row_x[t, row, k:k + 1, :] = jnp.sum(w.astype(F32), axis=0, keepdims=True)

        share = nb // cols

        def q_loop(r, carry):
            w = lax.dot_general(c_nm[...], data_f[r], NN, preferred_element_type=F32)
            q_b[:, :, :, lanes(r)] = w.astype(BF16).reshape(zh_n, 2, share, kd)
            remote(q_b.at[:, 1 - c, :, lanes(r)], q_r.at[:, :, lanes(r)],
                   qsend.at[r], qrecv.at[r], col=c_p).start()
            return carry

        def q_sum(r, carry):
            landed(q_r.at[:, :, lanes(r)], qrecv.at[r])
            q_s[:, :, lanes(r)] = (
                q_b[:, c, :, lanes(r)].astype(F32) + q_r[:, :, lanes(r)].astype(F32)
            ).astype(BF16)
            return carry

        z_count = [0]

        def z_send(src, dst, sem, dev):
            k = z_count[0]
            z_count[0] += 1
            cp = remote(src, dst, zsend.at[k], sem, col=dev)
            cp.start()
            pending.append(cp)

        def wide_lanes(kk):
            return pl.ds(kk * wide, wide)

        def z_start(kk):
            at = wide_lanes(kk)
            z_send(q_s.at[far * 2, :, at], z_first.at[kk, 0], zrecv.at[kk, 0, 0], z_up)
            z_send(q_s.at[far * 2 + 1, :, at], z_first.at[kk, 1], zrecv.at[kk, 0, 1], z_dn)

        def z_add(s, kk, i, zi):
            ln = wide_lanes(kk)
            if s == 1:
                landed(z_first.at[kk, i], zrecv.at[kk, 0, i])
                at = (zi * 2 + i, slice(None), ln)
                q_s[at] = (q_s[at].astype(F32) + z_first[kk, i].astype(F32)).astype(BF16)
            else:
                landed(z_next.at[s - 2, kk, i], zrecv.at[kk, s - 1, i])
                at = (pl.ds(zi * 2, 2), slice(None), ln)
                q_s[at] = (q_s[at].astype(F32) + z_next[s - 2, kk, i].astype(F32)).astype(BF16)

        def z_step(s, kk):
            for i, sign, dev in ((0, 1, z_up), (1, -1, z_dn)):
                zi = zz(sign * (4 - s))
                z_add(s, kk, i, zi)
                z_send(q_s.at[pl.ds(zi * 2, 2), :, wide_lanes(kk)], z_next.at[s - 1, kk, i], zrecv.at[kk, s, i], dev)

        def z_end(kk):
            ln = wide_lanes(kk)
            for i in (0, 1):
                landed(z_next.at[2, kk, i], zrecv.at[kk, 3, i])
            own[:, :, ln] = (
                q_s[pl.ds(z * 2, 2), :, ln].astype(F32)
                + z_next[2, kk, 0].astype(F32) + z_next[2, kk, 1].astype(F32)
            )
            h_out[kk] = own[1 - h, :, ln].astype(BF16)
            z_send(h_out.at[kk], h_in.at[kk], hrecv.at[kk], h_p)

        def rest(k, carry):
            dx = jnp.where(k == 1, 1, 0)
            dy = jnp.where(k == 0, 2, jnp.where(k == 2, 1, jnp.where(k == 3, 3, 0)))
            p_dot(rid(dx, dy))
            return carry

        def add_to(r, i, ref):
            at = pl.ds(i * half, half)
            p_b[r, at, :] = (p_b[r, at, :].astype(F32) + ref.astype(F32)).astype(BF16)

        p_count = [0]

        def p_send(r, i, dst, sem, dev):
            k = p_count[0]
            p_count[0] += 1
            cp = remote(p_half_of(r, i), dst, p2send.at[k], sem, row=dev)
            cp.start()
            pending.append(cp)

        def opposite(i):
            landed(p_lead.at[2, i], precv.at[2, i])
            add_to(across, i, p_lead[2, i])
            p_send(across, i, p_half.at[i], p2recv.at[i], (y_up, y_dn)[i])

        def over_x(i):
            landed(p_lead.at[0, i], precv.at[0, i])
            landed(p_lead.at[1, i], precv.at[1, i])
            at = (x_p, pl.ds(i * half, half), slice(None))
            p_b[at] = (p_b[at].astype(F32) + p_lead[0, i].astype(F32) + p_lead[1, i].astype(F32)).astype(BF16)
            p_send(x_p, i, p_x.at[i], p2recv.at[2 + i], x_p)

        def beside():
            for i, r, dev in ((0, y_up, y_up), (1, y_dn, y_dn)):
                p_send(r, 1 - i, p_next.at[i, 1 - i], p2recv.at[4 + 2 * i], dev)
            for i, r, dev in ((0, y_up, y_up), (1, y_dn, y_dn)):
                landed(p_half.at[i], p2recv.at[i])
                add_to(r, i, p_half[i])
                p_send(r, i, p_next.at[i, i], p2recv.at[5 + 2 * i], dev)

        lax.fori_loop(0, 4, q_loop, 0)
        lax.fori_loop(0, 4, q_sum, 0)
        z_start(0)
        lax.fori_loop(4, 8, q_loop, 0)
        lax.fori_loop(4, 8, q_sum, 0)
        z_start(1)
        z_step(1, 0)
        lax.fori_loop(0, 5, rest, 0)
        opposite(0)
        z_step(1, 1)
        landed(core_x.at[t, 1 - c], core_recv.at[t])
        col_x[t, zh] = core_x[t, 0] + core_x[t, 1]
        start_col(t)
        start_row(t)
        z_step(2, 0)
        over_x(0)
        opposite(1)
        over_x(1)
        z_step(2, 1)
        z_step(3, 0)
        beside()
        z_step(3, 1)
        got_row(t)
        v_col[...] = column(1.0 / jnp.sum(row_x[t], axis=0))
        got_col(t)
        u_col[...] = column(1.0 / jnp.sum(col_x[t], axis=0))
        z_end(0)
        z_end(1)
        inv = u_col[pl.ds(pl.multiple_of(col * share, share), share), :]
        for kk in (0, 1):
            landed(h_in.at[kk], hrecv.at[kk])
            for k in range(wide // 128):
                at = slice(k * 128, (k + 1) * 128)
                to = slice(kk * wide + k * 128, kk * wide + (k + 1) * 128)
                nt_ref[:, to] = inv * (own[h, :, to] + h_in[kk, :, at].astype(F32))
        for i in (0, 1):
            at = pl.ds(i * half, half)
            landed(p_x.at[i], p2recv.at[2 + i])
            landed(p_next.at[0, i], p2recv.at[4 + (1 if i == 0 else 0)])
            landed(p_next.at[1, i], p2recv.at[6 + (1 if i == 1 else 0)])
            for k in range(kd // 128):
                ln = slice(k * 128, (k + 1) * 128)
                dt_ref[at, ln] = v_col[at, :] * (
                    p_b[row, at, ln].astype(F32) + p_x[i, :, ln].astype(F32)
                    + p_next[0, i, :, ln].astype(F32) + p_next[1, i, :, ln].astype(F32)
                )

    for cp in pending:
        cp.wait_send()
    for t in range(ITERS + 1):
        if (stage >= 2 and t < ITERS) or stage >= 3:
            landed(col_x.at[t, pl.ds(0, zh_n - 1)], col_send.at[t])
            landed(row_x.at[t, pl.ds(0, ROWS - 1)], row_send.at[t])
    if stage >= 3:
        for k in range(3):
            for i in (0, 1):
                landed(p_lead.at[k, i], psend.at[k, i])

        def left(r, carry):
            landed(q_r.at[:, :, lanes(r)], qsend.at[r])
            return carry

        lax.fori_loop(0, ROWS, left, 0)
    if stage < 3:
        nt_ref[...] = jnp.zeros_like(nt_ref)
        dt_ref[...] = s_nm[...] + s_mn[...]


def local(noise, data, stage=3, opts=()):
    nb, kn = noise.shape
    mb, kd = data.shape
    cols = 4 * ZN
    zh_n = 2 * ZN
    features = kd * ROWS
    wide = features // 2
    share = nb // cols
    half = mb // 2
    vm = pltpu.VMEM
    dma = pltpu.SemaphoreType.DMA
    ex = ITERS + 1
    scratch = [
        vm((cols, nb, kn), BF16), vm((ROWS, mb, kd), BF16),
        vm((nb, mb), F32), vm((mb, nb), F32), vm((nb, mb), BF16), vm((mb, nb), BF16),
        vm((nb, 128), F32), vm((mb, 128), F32), vm((nb, 128), F32), vm((mb, 128), F32),
        vm((nb // 128, 128), F32), vm((mb // 128, 128), F32),
        vm((ex, 2, nb // 128, 128), F32), vm((ex, zh_n, nb // 128, 128), F32), vm((ex, ROWS, mb // 128, 128), F32),
        vm((ROWS, mb, kd), BF16), vm((3, 2, half, kd), BF16), vm((2, half, kd), BF16),
        vm((2, half, kd), BF16), vm((2, 2, half, kd), BF16),
        vm((zh_n, 2, share, features), BF16), vm((zh_n, share, features), BF16), vm((zh_n, share, features), BF16),
        vm((2, 2, share, wide), BF16), vm((3, 2, 2, 2, share, wide), BF16),
        vm((2, share, wide), BF16), vm((2, share, wide), BF16), vm((2, share, features), F32),
        dma((64,)), dma((cols, 2)), dma((28,)), dma((ROWS, PARTS)),
        dma((ex,)), dma((ex,)), dma((ex,)), dma((ex,)), dma((ex,)), dma((ex,)),
        dma((3, 2)), dma((3, 2)), dma((8,)), dma((8,)), dma((ROWS,)), dma((ROWS,)),
        dma((18,)), dma((2, 4, 2)), dma((2,)),
    ]
    return pl.pallas_call(
        functools.partial(kernel, (stage, opts)),
        out_shape=(
            jax.ShapeDtypeStruct((share, features), F32),
            jax.ShapeDtypeStruct((mb, kd), F32),
        ),
        in_specs=[pl.BlockSpec(memory_space=pltpu.VMEM)] * 2,
        out_specs=[pl.BlockSpec(memory_space=pltpu.VMEM)] * 2,
        scratch_shapes=scratch,
        compiler_params=pltpu.CompilerParams(
            collective_id=0, has_side_effects=True, vmem_limit_bytes=56 * 1024 * 1024
        ),
    )(noise, data)


def solution(mesh, stage=3, opts=()):
    return jax.shard_map(
        functools.partial(local, stage=stage, opts=opts),
        mesh=mesh,
        in_specs=(P("row", "col"), P("col", "row")),
        out_specs=(P(("row", "col"), None), P("col", "row")),
        check_vma=False,
    )
```

```python
import functools
import math

import jax
import jax.numpy as jnp
from jax import lax
from jax.experimental import pallas as pl
from jax.experimental.pallas import tpu as pltpu
from jax.sharding import PartitionSpec as P

ITERS = 3
YN = 4
ROWS = 8
ZN = 8
PARTS = 4
KS = 4
MULTIPLIES = (
    ("lead0",),
    ("lead1",),
    ("lead2", "cnm"),
    ("q0",),
    ("q1",),
    ("q2",),
    ("q3", "qs0"),
    ("q4", "qs1", "z0_0"),
    ("q5", "qs2"),
    ("q6", "qs3", "z0_1"),
    ("q7", "qs4", "z1_0_0", "z1_0_1"),
    ("Pxp", "qs5"),
    ("Pac", "z0_2", "z1_1_1", "z1_1_0", "op_00", "ox_0", "qs7", "qs6", "z0_3", "z2_0_1", "z2_0_0", "op_10"),
    ("Pdn", "z1_2_1", "op_01"),
    ("Pown", "z1_2_0", "z2_1_0", "ox_1", "op_11", "z1_3_1", "z2_1_1"),
    ("Pup",),
)
REST = (
    "na_0", "z1_3_0", "z2_2_0", "z3_0_0", "na_1", "z2_2_1", "z3_0_1", "z3_1_1", "z3_1_0", "nb_01", "z2_3_0",
    "z2_3_1", "massgo", "z3_2_1", "nb_00", "z3_2_0", "ze_0", "nb_10", "ze_1", "nb_11", "z3_3_0", "z3_3_1", "ze_2",
    "mass", "hf_0", "hf_1", "ze_3", "hf_2", "f_0", "f_1", "hf_3",
)
MESH = pl.DeviceIdType.MESH
F32 = jnp.float32
BF16 = jnp.bfloat16
NT = (((1,), (1,)), ((), ()))
NN = (((1,), (0,)), ((), ()))


def remote(src, dst, send, recv, **dev):
    return pltpu.make_async_remote_copy(
        src_ref=src, dst_ref=dst, send_sem=send, recv_sem=recv,
        device_id=dev, device_id_type=MESH,
    )


def landed(ref, sem):
    pltpu.make_async_copy(ref, ref, sem).wait()


def column(rows4):
    blocks = [
        jnp.transpose(jnp.broadcast_to(rows4[k:k + 1, :], (128, 128)))
        for k in range(rows4.shape[0])
    ]
    return jnp.concatenate(blocks, axis=0)


def local_lse(mat, col, out):
    for k in range(mat.shape[1] // 128):
        x = col[...] - mat[:, k * 128:(k + 1) * 128]
        m = jnp.max(x, axis=0, keepdims=True)
        s = jnp.sum(jnp.exp2(x - m), axis=0, keepdims=True)
        out[k:k + 1, :] = m + jnp.log2(s)


def combine(parts):
    top = jnp.max(parts, axis=0)
    return top + jnp.log2(jnp.sum(jnp.exp2(parts - top[None]), axis=0))


def kernel(
    cfg, noise_hbm, data_hbm, nt_ref, dt_ref, noise_ref, data_ref, in_sem,
    noise_f, data_f, s_nm, s_mn, c_nm, c_mn, u_col, v_col, sq_n, sq_m, u_row, v_row,
    core_x, col_x, row_x,
    p_b, p_lead, p_half, p_x, p_next, q_b, q_r, q_s, z_first, z_next, h_out, h_in, own,
    nsend, nrecv, dsend, drecv,
    core_send, core_recv, col_send, col_recv, row_send, row_recv,
    psend, precv, xqsend, xqrecv, p2send, p2recv, qsend, qrecv, zsend, zrecv, hrecv,
):
    stage, opts = cfg
    zn = ZN
    nb = noise_ref.shape[0]
    mb = data_ref.shape[0]
    kd = data_ref.shape[1]
    kn = noise_ref.shape[1]
    cols = 4 * zn
    npp = cols // ROWS
    zh_n = 2 * zn
    half = mb // 2
    part = mb // PARTS
    fold = nb // 2
    features = kd * ROWS
    scale = math.log2(math.e) / (0.25 * features)
    log_rows = math.log2(nb * ROWS)
    log_cols = math.log2(mb * cols)

    row = lax.axis_index("row")
    col = lax.axis_index("col")
    xl = lax.div(row, YN)
    y = lax.rem(row, YN)
    z = lax.div(col, 4)
    h = lax.rem(lax.div(col, 2), 2)
    c = lax.rem(col, 2)

    def rid(dx, dy):
        return lax.rem(xl + dx, 2) * YN + lax.rem(y + dy, YN)

    def zz(d):
        return lax.rem(z + d + zn, zn)

    def cid(zi, hi, ci):
        return (zi * 2 + hi) * 2 + ci

    y_up, y_dn, x_p = rid(0, 1), rid(0, 3), rid(1, 0)
    z_up, z_dn = cid(zz(1), h, c), cid(zz(-1), h, c)
    h_p = cid(z, 1 - h, c)
    c_p = cid(z, h, 1 - c)
    zh = z * 2 + h

    barrier = pltpu.get_barrier_semaphore()

    def greet(**dev):
        pl.semaphore_signal(barrier, inc=1, device_id=dev, device_id_type=MESH)

    for dev in (y_up, y_dn, x_p):
        greet(row=dev)
    for dev in (z_up, z_dn, h_p, c_p):
        greet(col=dev)
    loads = [pltpu.make_async_copy(noise_hbm, noise_ref, in_sem.at[0])]
    for i in range(PARTS):
        at = pl.ds(i * part, part)
        loads.append(pltpu.make_async_copy(data_hbm.at[at], data_ref.at[at], in_sem.at[1 + i]))
    for cp in loads:
        cp.start()
    loads[0].wait()
    noise_f[col] = noise_ref[...].astype(BF16)
    for i in range(PARTS):
        loads[1 + i].wait()
        data_f[row, i * part:(i + 1) * part, :] = data_ref[i * part:(i + 1) * part, :].astype(BF16)
    pl.semaphore_wait(barrier, 7)

    pending = []
    n_count = [0]
    d_count = [0]

    def noise_part(piece, i):
        return noise_f.at[piece, pl.ds(i * fold, fold), :]

    def send_noise(piece, i, dev):
        k = n_count[0]
        n_count[0] += 1
        ref = noise_f.at[piece] if i is None else noise_part(piece, i)
        cp = remote(ref, ref, nsend.at[k], nrecv.at[piece, 0 if i is None else i], col=dev)
        cp.start()
        pending.append(cp)

    def got_noise(piece, i):
        ref = noise_f.at[piece] if i is None else noise_part(piece, i)
        landed(ref, nrecv.at[piece, 0 if i is None else i])

    def data_part(r, i):
        return data_f.at[r, pl.ds(i * part, part), :]

    def send_data(r, i, dev):
        k = d_count[0]
        d_count[0] += 1
        cp = remote(data_part(r, i), data_part(r, i), dsend.at[k], drecv.at[r, i], row=dev)
        cp.start()
        pending.append(cp)

    def got_data(r, i):
        landed(data_part(r, i), drecv.at[r, i])

    across = rid(0, 2)
    for i in (0, 1):
        send_noise(col, i, h_p)
        send_noise(col, i, z_up)
        send_noise(col, i, z_dn)
        send_data(row, i, y_up)
        send_data(row, i + 2, y_dn)
        send_data(row, i, x_p)
    send_data(row, 2, y_up)
    send_data(row, 0, y_dn)
    send_data(row, 2, x_p)
    send_data(row, 3, x_p)
    send_noise(col, None, c_p)

    def noise_got(s, hi, i):
        up, dn = cid(zz(-s), hi, c), cid(zz(s), hi, c)
        got_noise(up, i)
        if s < 3 or i == 0:
            send_noise(up, i, z_up)
        got_noise(dn, i)
        if s < 3 or i == 1:
            send_noise(dn, i, z_dn)
        if i == 1:
            send_noise(up, None, c_p)
            send_noise(dn, None, c_p)

    def noise_pair(i):
        got_noise(h_p, i)
        send_noise(h_p, i, z_up)
        send_noise(h_p, i, z_dn)
        if i == 1:
            send_noise(h_p, None, c_p)

    def pass_on(i):
        got_data(y_dn, i)
        send_data(y_dn, i, y_up)
        got_data(y_up, i + 2)
        send_data(y_up, i + 2, y_dn)

    def from_x(i):
        got_data(x_p, i)
        send_data(x_p, i, y_up)
        send_data(x_p, i, y_dn)

    def to_x(i):
        for k in (i, i + 2):
            got_data(across, k)
            send_data(across, k, x_p)

    g = 1 - h
    noise_got(1, h, 0)
    noise_pair(0)
    pass_on(0)
    noise_got(1, h, 1)
    noise_pair(1)
    noise_got(2, h, 0)
    pass_on(1)
    send_data(row, 3, y_up)
    send_data(row, 1, y_dn)
    from_x(0)
    noise_got(2, h, 1)
    noise_got(1, g, 0)
    from_x(1)
    noise_got(3, h, 0)
    noise_got(1, g, 1)
    noise_got(3, h, 1)
    from_x(2)
    to_x(0)
    noise_got(2, g, 0)
    from_x(3)
    to_x(1)
    noise_got(2, g, 1)
    noise_got(3, g, 0)
    noise_got(3, g, 1)
    for i in (2, 3):
        got_data(y_dn, i)
        got_data(y_up, i - 2)

    s_nm[...] = jnp.zeros_like(s_nm)
    s_mn[...] = jnp.zeros_like(s_mn)
    sq_n[...] = jnp.zeros_like(sq_n)
    sq_m[...] = jnp.zeros_like(sq_m)

    def noise_cat(r):
        return jnp.concatenate([noise_f[r * npp + i] for i in range(npp)], axis=1)

    def squares(sq, at, v):
        total = sq[at, :]
        for i in range(v.shape[1] // 128):
            w = v[:, i * 128:(i + 1) * 128].astype(F32)
            total += w * w
        sq[at, :] = total

    def chunk(r, k=None):
        at = pl.ds(0, mb) if k is None else pl.ds(k * half, half)
        a = noise_cat(r)
        d = data_f[r, at, :]
        s_nm[:, at] += lax.dot_general(a, d, NT, preferred_element_type=F32)
        s_mn[at, :] += lax.dot_general(d, a, NT, preferred_element_type=F32)
        squares(sq_m, at, d)
        if k != 1:
            squares(sq_n, pl.ds(0, nb), a)

    def plane(k):
        step = lax.div(k + 1, 2)
        zi = zz(jnp.where(lax.rem(k, 2) == 0, step, -step))
        for hi in (0, 1):
            got_noise(cid(zi, hi, 1 - c), None)

        @pl.when((lax.div(zi, YN) == xl) | (lax.rem(zi, YN) == y))
        def _():
            chunk(zi)

    def near_plane(k, carry):
        plane(k)
        return carry

    lax.fori_loop(0, 5, near_plane, 0)
    far = zz(4)
    for hi in (0, 1):
        for i in (0, 1):
            got_noise(cid(far, hi, c), i)
        send_noise(cid(far, hi, c), None, c_p)
    lax.fori_loop(5, 8, near_plane, 0)

    def sides(k):
        def body(j, carry):
            r = rid(1, jnp.where(j == 0, 1, 3))
            for i in (2 * k, 2 * k + 1):
                got_data(r, i)
            chunk(r, k)
            return carry

        lax.fori_loop(0, 2, body, 0)

    sides(0)
    for i in range(PARTS):
        got_data(rid(1, 2), i)
    chunk(rid(1, 2))
    sides(1)

    def rows_of(sq):
        t = jnp.sum(jnp.transpose(sq), axis=0, keepdims=True)
        return jnp.concatenate([t[:, k * 128:(k + 1) * 128] for k in range(t.shape[1] // 128)], axis=0)

    ns = rows_of(sq_n[...])
    ds = rows_of(sq_m[...])
    u_col[...] = column(ns)
    v_col[...] = column(ds)
    for k in range(mb // 128):
        at = (slice(None), slice(k * 128, (k + 1) * 128))
        s_nm[at] = (u_col[...] + ds[k:k + 1, :] - 2.0 * s_nm[at]) * scale
    for k in range(nb // 128):
        at = (slice(None), slice(k * 128, (k + 1) * 128))
        s_mn[at] = (v_col[...] + ns[k:k + 1, :] - 2.0 * s_mn[at]) * scale

    col_to = [cid(zz(d), hi, c) for d in (4, 3, -3, 2, -2, 1, -1, 0) for hi in (1 - h, h)][:-1]
    row_to = [rid(dx, dy) for dy in (2, 1, 3, 0) for dx in (1, 0)][:-1]

    def start_core(t):
        cp = remote(core_x.at[t, c], core_x.at[t, c], core_send.at[t], core_recv.at[t], col=c_p)
        cp.start()
        pending.append(cp)

    def start_col(t):
        for to in col_to:
            remote(col_x.at[t, zh], col_x.at[t, zh], col_send.at[t], col_recv.at[t], col=to).start()

    def start_row(t):
        for to in row_to:
            remote(row_x.at[t, row], row_x.at[t, row], row_send.at[t], row_recv.at[t], row=to).start()

    def got_col(t):
        landed(col_x.at[t, pl.ds(0, zh_n - 1)], col_recv.at[t])

    def got_row(t):
        landed(row_x.at[t, pl.ds(0, ROWS - 1)], row_recv.at[t])

    if stage >= 2:
        v_col[...] = jnp.zeros_like(v_col)
        for t in range(ITERS):
            local_lse(s_mn, v_col, core_x.at[t, c])
            start_core(t)
            landed(core_x.at[t, 1 - c], core_recv.at[t])
            col_x[t, zh] = combine(core_x[t])
            start_col(t)
            got_col(t)
            u = -(combine(col_x[t]) + log_rows)
            u_row[...] = u
            u_col[...] = column(u)
            local_lse(s_nm, u_col, row_x.at[t, row])
            start_row(t)
            got_row(t)
            v = -(combine(row_x[t]) + log_cols)
            v_row[...] = v
            v_col[...] = column(v)

    wide = features // KS

    def lanes(r):
        return pl.ds(pl.multiple_of(r * kd, kd), kd)

    if stage >= 3:
        t = ITERS
        logs = log_rows + log_cols
        for k in range(nb // 128):
            at = (slice(None), slice(k * 128, (k + 1) * 128))
            w = jnp.exp2(v_col[...] + u_row[k:k + 1, :] - s_mn[at] + logs).astype(BF16)
            c_mn[at] = w
            core_x[t, c, k:k + 1, :] = jnp.sum(w.astype(F32), axis=0, keepdims=True)
        start_core(t)

        def p_dot(r):
            p_b[r] = lax.dot_general(c_mn[...], noise_cat(r), NN, preferred_element_type=F32).astype(BF16)

        quarter = half // 2

        def p_rows(r, first, count):
            return p_b.at[r, pl.ds(first, count), :]

        leaving = []
        steps = {}

        def leave(src, to, send, recv, **dev):
            remote(src, to[0].at[to[1]], send[0].at[send[1]], recv, **dev).start()
            leaving.append((to, send))

        def lead(k):
            r, dev = ((rid(1, 1), y_up), (rid(1, 3), y_dn), (rid(1, 2), x_p))[k]
            if k < 2:
                for i in (0, 1):
                    leave(p_rows(r, i * half, half), (p_lead, (k, i)), (psend, (k, i)), precv.at[k, i], row=dev)
            else:
                for j in (0, 1):
                    for i in (0, 1):
                        to = (p_lead, (2, i, pl.ds(j * quarter, quarter)))
                        src = p_rows(r, i * half + j * quarter, quarter)
                        leave(src, to, (xqsend, (i, j)), xqrecv.at[i, j], row=dev)

        def coupling():
            for k in range(mb // 128):
                at = (slice(None), slice(k * 128, (k + 1) * 128))
                w = jnp.exp2(u_col[...] + v_row[k:k + 1, :] - s_nm[at] + logs).astype(BF16)
                c_nm[at] = w
                row_x[t, row, k:k + 1, :] = jnp.sum(w.astype(F32), axis=0, keepdims=True)
            start_row(t)

        steps["cnm"] = coupling
        share = nb // cols

        def q_dot(r):
            w = lax.dot_general(c_nm[...], data_f[r], NN, preferred_element_type=F32)
            q_b[:, :, :, lanes(r)] = w.astype(BF16).reshape(zh_n, 2, share, kd)
            remote(q_b.at[:, 1 - c, :, lanes(r)], q_r.at[:, :, lanes(r)],
                   qsend.at[r], qrecv.at[r], col=c_p).start()

        def q_sum(r):
            landed(q_r.at[:, :, lanes(r)], qrecv.at[r])
            q_s[:, :, lanes(r)] = (
                q_b[:, c, :, lanes(r)].astype(F32) + q_r[:, :, lanes(r)].astype(F32)
            ).astype(BF16)

        for r in range(ROWS):
            steps["qs%d" % r] = functools.partial(q_sum, r)

        z_count = [0]

        def z_send(src, dst, sem, dev):
            k = z_count[0]
            z_count[0] += 1
            leave(src, dst, (zsend, k), sem, col=dev)

        def wide_lanes(kk):
            return pl.ds(kk * wide, wide)

        def z_start(kk):
            at = wide_lanes(kk)
            z_send(q_s.at[far * 2, :, at], (z_first, (kk, 0)), zrecv.at[kk, 0, 0], z_up)
            z_send(q_s.at[far * 2 + 1, :, at], (z_first, (kk, 1)), zrecv.at[kk, 0, 1], z_dn)

        def z_add(s, kk, i, zi):
            ln = wide_lanes(kk)
            if s == 1:
                landed(z_first.at[kk, i], zrecv.at[kk, 0, i])
                at = (zi * 2 + i, slice(None), ln)
                q_s[at] = (q_s[at].astype(F32) + z_first[kk, i].astype(F32)).astype(BF16)
            else:
                landed(z_next.at[s - 2, kk, i], zrecv.at[kk, s - 1, i])
                at = (pl.ds(zi * 2, 2), slice(None), ln)
                q_s[at] = (q_s[at].astype(F32) + z_next[s - 2, kk, i].astype(F32)).astype(BF16)

        def z_step(s, kk, i):
            sign, dev = ((1, z_up), (-1, z_dn))[i]
            zi = zz(sign * (4 - s))
            z_add(s, kk, i, zi)
            z_send(q_s.at[pl.ds(zi * 2, 2), :, wide_lanes(kk)], (z_next, (s - 1, kk, i)), zrecv.at[kk, s, i], dev)

        def z_end(kk):
            ln = wide_lanes(kk)
            for i in (0, 1):
                landed(z_next.at[2, kk, i], zrecv.at[kk, 3, i])
            own[:, :, ln] = (
                q_s[pl.ds(z * 2, 2), :, ln].astype(F32)
                + z_next[2, kk, 0].astype(F32) + z_next[2, kk, 1].astype(F32)
            )
            h_out[kk] = own[1 - h, :, ln].astype(BF16)
            z_send(h_out.at[kk], (h_in, kk), hrecv.at[kk], h_p)

        for kk in range(KS):
            steps["z0_%d" % kk] = functools.partial(z_start, kk)
            steps["ze_%d" % kk] = functools.partial(z_end, kk)
            for st in (1, 2, 3):
                for i in (0, 1):
                    steps["z%d_%d_%d" % (st, kk, i)] = functools.partial(z_step, st, kk, i)

        p_count = [0]

        def p_send(src, dst, sem, dev):
            k = p_count[0]
            p_count[0] += 1
            leave(src, dst, (p2send, k), p2recv.at[sem], row=dev)

        def add_to(r, first, count, refs):
            at = (r, pl.ds(first, count), slice(None))
            total = p_b[at].astype(F32)
            for ref in refs:
                total += ref[...].astype(F32)
            p_b[at] = total.astype(BF16)

        def opposite(i, j):
            ref = p_lead.at[2, i, pl.ds(j * quarter, quarter)]
            landed(ref, xqrecv.at[i, j])
            first = i * half + j * quarter
            add_to(across, first, quarter, [ref])
            p_send(p_rows(across, first, quarter), (p_half, (i, j)), 2 * i + j, (y_up, y_dn)[i])

        def over_x(i):
            for k in (0, 1):
                landed(p_lead.at[k, i], precv.at[k, i])
            add_to(x_p, i * half, half, [p_lead.at[0, i], p_lead.at[1, i]])
            p_send(p_rows(x_p, i * half, half), (p_x, i), 4 + i, x_p)

        def beside(i):
            dev = (y_up, y_dn)[i]
            p_send(p_rows(dev, (1 - i) * half, half), (p_next, (i, 1 - i)), 6 + i, dev)

        def beside_sum(i, j):
            dev = (y_up, y_dn)[i]
            landed(p_half.at[i, j], p2recv.at[2 * i + j])
            first = i * half + j * quarter
            add_to(dev, first, quarter, [p_half.at[i, j]])
            p_send(p_rows(dev, first, quarter), (p_next, (i, i, pl.ds(j * quarter, quarter))), 8 + 2 * i + j, dev)

        def send_masses():
            landed(core_x.at[t, 1 - c], core_recv.at[t])
            col_x[t, zh] = core_x[t, 0] + core_x[t, 1]
            start_col(t)

        def masses():
            got_row(t)
            v_col[...] = column(1.0 / jnp.sum(row_x[t], axis=0))
            got_col(t)
            u_col[...] = column(1.0 / jnp.sum(col_x[t], axis=0))

        def noise_out(kk):
            inv = u_col[pl.ds(pl.multiple_of(col * share, share), share), :]
            landed(h_in.at[kk], hrecv.at[kk])
            for k in range(wide // 128):
                at = slice(k * 128, (k + 1) * 128)
                to = slice(kk * wide + k * 128, kk * wide + (k + 1) * 128)
                nt_ref[:, to] = inv * (own[h, :, to] + h_in[kk, :, at].astype(F32))

        def data_out(i):
            at = pl.ds(i * half, half)
            landed(p_x.at[i], p2recv.at[4 + i])
            landed(p_next.at[1 - i, i], p2recv.at[7 - i])
            for j in (0, 1):
                landed(p_next.at[i, i, pl.ds(j * quarter, quarter)], p2recv.at[8 + 2 * i + j])
            for k in range(kd // 128):
                ln = slice(k * 128, (k + 1) * 128)
                dt_ref[at, ln] = v_col[at, :] * (
                    p_b[row, at, ln].astype(F32) + p_x[i, :, ln].astype(F32)
                    + p_next[0, i, :, ln].astype(F32) + p_next[1, i, :, ln].astype(F32)
                )

        steps["massgo"] = send_masses
        steps["mass"] = masses
        for i in (0, 1):
            for j in (0, 1):
                steps["op_%d%d" % (i, j)] = functools.partial(opposite, i, j)
                steps["nb_%d%d" % (i, j)] = functools.partial(beside_sum, i, j)
            steps["ox_%d" % i] = functools.partial(over_x, i)
            steps["na_%d" % i] = functools.partial(beside, i)
            steps["f_%d" % i] = functools.partial(data_out, i)
        for kk in range(KS):
            steps["hf_%d" % kk] = functools.partial(noise_out, kk)

        blocks = dict(lead0=rid(1, 1), lead1=rid(1, 3), lead2=rid(1, 2),
                      Pac=across, Pxp=x_p, Pup=y_up, Pdn=y_dn, Pown=row)
        for k in range(3):
            steps["lead%d" % k] = functools.partial(lead, k)

        def multiply(k, carry):
            r = blocks[MULTIPLIES[0][0]]
            for_noise = k < 0
            for i, (name, *_) in enumerate(MULTIPLIES):
                if name in blocks:
                    r = jnp.where(k == i, blocks[name], r)
                else:
                    r = jnp.where(k == i, int(name[1:]), r)
                    for_noise = for_noise | (k == i)

            @pl.when(for_noise)
            def _():
                q_dot(r)

            @pl.when(jnp.logical_not(for_noise))
            def _():
                p_dot(r)

            for i, (name, *after) in enumerate(MULTIPLIES):
                after = ([name] if name.startswith("lead") else []) + after
                if after:
                    @pl.when(k == i)
                    def _(after=after):
                        for step in after:
                            steps[step]()
            return carry

        lax.fori_loop(0, len(MULTIPLIES), multiply, 0)
        for step in REST:
            steps[step]()
        for r in range(ROWS):
            landed(q_r.at[:, :, lanes(r)], qsend.at[r])
        for to, send in leaving:
            landed(to[0].at[to[1]], send[0].at[send[1]])

    for cp in pending:
        cp.wait_send()
    for t in range(ITERS + 1):
        if (stage >= 2 and t < ITERS) or stage >= 3:
            landed(col_x.at[t, pl.ds(0, zh_n - 1)], col_send.at[t])
            landed(row_x.at[t, pl.ds(0, ROWS - 1)], row_send.at[t])
    if stage < 3:
        nt_ref[...] = jnp.zeros_like(nt_ref)
        dt_ref[...] = s_nm[...] + s_mn[...]


def finish(n_in, d_in, n_out, d_out, sems):
    copies = [pltpu.make_async_copy(n_in, n_out, sems.at[0]), pltpu.make_async_copy(d_in, d_out, sems.at[1])]
    for cp in copies:
        cp.start()
    for cp in copies:
        cp.wait()


def local(noise, data, stage=3, opts=()):
    nb, kn = noise.shape
    mb, kd = data.shape
    cols = 4 * ZN
    zh_n = 2 * ZN
    features = kd * ROWS
    wide = features // KS
    share = nb // cols
    half = mb // 2
    vm = pltpu.VMEM
    dma = pltpu.SemaphoreType.DMA
    ex = ITERS + 1
    scratch = [
        vm(noise.shape, F32), vm(data.shape, F32), dma((1 + PARTS,)),
        vm((cols, nb, kn), BF16), vm((ROWS, mb, kd), BF16),
        vm((nb, mb), F32), vm((mb, nb), F32), vm((nb, mb), BF16), vm((mb, nb), BF16),
        vm((nb, 128), F32), vm((mb, 128), F32), vm((nb, 128), F32), vm((mb, 128), F32),
        vm((nb // 128, 128), F32), vm((mb // 128, 128), F32),
        vm((ex, 2, nb // 128, 128), F32), vm((ex, zh_n, nb // 128, 128), F32), vm((ex, ROWS, mb // 128, 128), F32),
        vm((ROWS, mb, kd), BF16), vm((3, 2, half, kd), BF16), vm((2, 2, half // 2, kd), BF16),
        vm((2, half, kd), BF16), vm((2, 2, half, kd), BF16),
        vm((zh_n, 2, share, features), BF16), vm((zh_n, share, features), BF16), vm((zh_n, share, features), BF16),
        vm((KS, 2, share, wide), BF16), vm((3, KS, 2, 2, share, wide), BF16),
        vm((KS, share, wide), BF16), vm((KS, share, wide), BF16), vm((2, share, features), F32),
        dma((64,)), dma((cols, 2)), dma((28,)), dma((ROWS, PARTS)),
        dma((ex,)), dma((ex,)), dma((ex,)), dma((ex,)), dma((ex,)), dma((ex,)),
        dma((2, 2)), dma((2, 2)), dma((2, 2)), dma((2, 2)), dma((12,)), dma((12,)), dma((ROWS,)), dma((ROWS,)),
        dma((9 * KS,)), dma((KS, 4, 2)), dma((KS,)),
    ]
    sums = pl.pallas_call(
        functools.partial(kernel, (stage, opts)),
        out_shape=(
            pltpu.VMEM((share, features), F32),
            pltpu.VMEM((mb, kd), F32),
        ),
        in_specs=[pl.BlockSpec(memory_space=pltpu.HBM)] * 2,
        out_specs=[pl.BlockSpec(memory_space=pltpu.VMEM)] * 2,
        scratch_shapes=scratch,
        compiler_params=pltpu.CompilerParams(
            collective_id=0, has_side_effects=True, vmem_limit_bytes=125 * 512 * 1024
        ),
    )(noise, data)
    if "nofin" in opts:
        return sums
    return pl.pallas_call(
        finish,
        out_shape=tuple(jax.ShapeDtypeStruct(v.shape, v.dtype) for v in sums),
        in_specs=[pl.BlockSpec(memory_space=pltpu.VMEM)] * 2,
        out_specs=[pl.BlockSpec(memory_space=pl.ANY)] * 2,
        scratch_shapes=[dma((2,))],
        compiler_params=pltpu.CompilerParams(vmem_limit_bytes=8 * 1024 * 1024),
    )(*sums)


def solution(mesh, stage=3, opts=()):
    return jax.shard_map(
        functools.partial(local, stage=stage, opts=opts),
        mesh=mesh,
        in_specs=(P("row", "col"), P("col", "row")),
        out_specs=(P(("row", "col"), None), P("col", "row")),
        check_vma=False,
    )
```

```python
import functools
import math

import jax
import jax.numpy as jnp
from jax import lax
from jax.experimental import pallas as pl
from jax.experimental.pallas import tpu as pltpu
from jax.sharding import PartitionSpec as P

ITERS = 3
YN = 4
ROWS = 8
ZN = 8
PARTS = 4
KS = 4
MULTIPLIES = (
    ("lead0",),
    ("lead1",),
    ("lead2", "cnm"),
    ("q0",),
    ("q1",),
    ("q2",),
    ("q3", "massgo", "qs0"),
    ("q4", "qs1", "z0_0"),
    ("q5", "qs2"),
    ("q6", "qs3", "z0_1"),
    ("q7", "qs4", "z1_0_0", "z1_0_1"),
    ("Pxp", "qs5"),
    ("Pac", "z0_2", "z1_1_1", "z1_1_0", "op_00", "ox_0", "qs7", "qs6", "z0_3", "z2_0_1", "z2_0_0", "op_10"),
    ("Pdn", "z1_2_1", "op_01"),
    ("Pown", "z1_2_0", "z2_1_0", "ox_1", "op_11", "z1_3_1", "z2_1_1"),
    ("Pup",),
)
REST = (
    "na_0", "z1_3_0", "z2_2_0", "z3_0_0", "na_1", "z2_2_1", "z3_0_1", "z3_1_1", "z3_1_0", "nb_01", "z2_3_0",
    "z2_3_1", "z3_2_1", "nb_00", "z3_2_0", "ze_0", "nb_10", "ze_1", "nb_11", "z3_3_0", "z3_3_1", "ze_2",
    "mass", "hf_0", "hf_1", "ze_3", "hf_2", "f_0", "f_1", "hf_3",
)
MESH = pl.DeviceIdType.MESH
F32 = jnp.float32
BF16 = jnp.bfloat16
NT = (((1,), (1,)), ((), ()))
NN = (((1,), (0,)), ((), ()))


def remote(src, dst, send, recv, **dev):
    return pltpu.make_async_remote_copy(
        src_ref=src, dst_ref=dst, send_sem=send, recv_sem=recv,
        device_id=dev, device_id_type=MESH,
    )


def landed(ref, sem):
    pltpu.make_async_copy(ref, ref, sem).wait()


def column(rows4):
    blocks = [
        jnp.transpose(jnp.broadcast_to(rows4[k:k + 1, :], (128, 128)))
        for k in range(rows4.shape[0])
    ]
    return jnp.concatenate(blocks, axis=0)


def local_lse(mat, col, out):
    for k in range(mat.shape[1] // 128):
        x = col[...] - mat[:, k * 128:(k + 1) * 128]
        m = jnp.max(x, axis=0, keepdims=True)
        s = jnp.sum(jnp.exp2(x - m), axis=0, keepdims=True)
        out[k:k + 1, :] = m + jnp.log2(s)


def combine(parts):
    top = jnp.max(parts, axis=0)
    return top + jnp.log2(jnp.sum(jnp.exp2(parts - top[None]), axis=0))


def kernel(
    cfg, noise_hbm, data_hbm, nt_ref, dt_ref, noise_ref, data_ref, in_sem,
    noise_f, data_f, s_nm, s_mn, c_nm, c_mn, u_col, v_col, sq_n, sq_m, u_row, v_row,
    core_x, col_x, row_x,
    p_b, p_lead, p_half, p_x, p_next, q_b, q_r, q_s, z_first, z_next, h_out, h_in, own,
    nsend, nrecv, dsend, drecv,
    core_send, core_recv, col_send, col_recv, row_send, row_recv,
    psend, precv, xqsend, xqrecv, p2send, p2recv, qsend, qrecv, zsend, zrecv, hrecv,
):
    stage, opts = cfg
    zn = ZN
    nb = noise_ref.shape[0]
    mb = data_ref.shape[0]
    kd = data_ref.shape[1]
    kn = noise_ref.shape[1]
    cols = 4 * zn
    npp = cols // ROWS
    zh_n = 2 * zn
    half = mb // 2
    part = mb // PARTS
    fold = nb // 2
    features = kd * ROWS
    scale = math.log2(math.e) / (0.25 * features)
    log_rows = math.log2(nb * ROWS)
    log_cols = math.log2(mb * cols)

    row = lax.axis_index("row")
    col = lax.axis_index("col")
    xl = lax.div(row, YN)
    y = lax.rem(row, YN)
    z = lax.div(col, 4)
    h = lax.rem(lax.div(col, 2), 2)
    c = lax.rem(col, 2)

    def rid(dx, dy):
        return lax.rem(xl + dx, 2) * YN + lax.rem(y + dy, YN)

    def zz(d):
        return lax.rem(z + d + zn, zn)

    def cid(zi, hi, ci):
        return (zi * 2 + hi) * 2 + ci

    y_up, y_dn, x_p = rid(0, 1), rid(0, 3), rid(1, 0)
    z_up, z_dn = cid(zz(1), h, c), cid(zz(-1), h, c)
    h_p = cid(z, 1 - h, c)
    c_p = cid(z, h, 1 - c)
    zh = z * 2 + h

    barrier = pltpu.get_barrier_semaphore()

    def greet(**dev):
        pl.semaphore_signal(barrier, inc=1, device_id=dev, device_id_type=MESH)

    for dev in (y_up, y_dn, x_p):
        greet(row=dev)
    for dev in (z_up, z_dn, h_p, c_p):
        greet(col=dev)
    loads = [pltpu.make_async_copy(noise_hbm, noise_ref, in_sem.at[0])]
    for i in range(PARTS):
        at = pl.ds(i * part, part)
        loads.append(pltpu.make_async_copy(data_hbm.at[at], data_ref.at[at], in_sem.at[1 + i]))
    for cp in loads:
        cp.start()
    loads[0].wait()
    noise_f[col] = noise_ref[...].astype(BF16)
    for i in range(PARTS):
        loads[1 + i].wait()
        data_f[row, i * part:(i + 1) * part, :] = data_ref[i * part:(i + 1) * part, :].astype(BF16)
    pl.semaphore_wait(barrier, 7)

    pending = []
    n_count = [0]
    d_count = [0]

    def noise_part(piece, i):
        return noise_f.at[piece, pl.ds(i * fold, fold), :]

    def send_noise(piece, i, dev):
        k = n_count[0]
        n_count[0] += 1
        ref = noise_f.at[piece] if i is None else noise_part(piece, i)
        cp = remote(ref, ref, nsend.at[k], nrecv.at[piece, 0 if i is None else i], col=dev)
        cp.start()
        pending.append(cp)

    def got_noise(piece, i):
        ref = noise_f.at[piece] if i is None else noise_part(piece, i)
        landed(ref, nrecv.at[piece, 0 if i is None else i])

    def data_part(r, i):
        return data_f.at[r, pl.ds(i * part, part), :]

    def send_data(r, i, dev):
        k = d_count[0]
        d_count[0] += 1
        cp = remote(data_part(r, i), data_part(r, i), dsend.at[k], drecv.at[r, i], row=dev)
        cp.start()
        pending.append(cp)

    def got_data(r, i):
        landed(data_part(r, i), drecv.at[r, i])

    across = rid(0, 2)
    for i in (0, 1):
        send_noise(col, i, h_p)
        send_noise(col, i, z_up)
        send_noise(col, i, z_dn)
        send_data(row, i, y_up)
        send_data(row, i + 2, y_dn)
        send_data(row, i, x_p)
    send_data(row, 2, y_up)
    send_data(row, 0, y_dn)
    send_data(row, 2, x_p)
    send_data(row, 3, x_p)
    send_noise(col, None, c_p)

    def noise_got(s, hi, i):
        up, dn = cid(zz(-s), hi, c), cid(zz(s), hi, c)
        got_noise(up, i)
        if s < 3 or i == 0:
            send_noise(up, i, z_up)
        got_noise(dn, i)
        if s < 3 or i == 1:
            send_noise(dn, i, z_dn)
        if i == 1:
            send_noise(up, None, c_p)
            send_noise(dn, None, c_p)

    def noise_pair(i):
        got_noise(h_p, i)
        send_noise(h_p, i, z_up)
        send_noise(h_p, i, z_dn)
        if i == 1:
            send_noise(h_p, None, c_p)

    def pass_on(i):
        got_data(y_dn, i)
        send_data(y_dn, i, y_up)
        got_data(y_up, i + 2)
        send_data(y_up, i + 2, y_dn)

    def from_x(i):
        got_data(x_p, i)
        send_data(x_p, i, y_up)
        send_data(x_p, i, y_dn)

    def to_x(i):
        for k in (i, i + 2):
            got_data(across, k)
            send_data(across, k, x_p)

    g = 1 - h
    noise_got(1, h, 0)
    noise_pair(0)
    pass_on(0)
    noise_got(1, h, 1)
    noise_pair(1)
    noise_got(2, h, 0)
    pass_on(1)
    send_data(row, 3, y_up)
    send_data(row, 1, y_dn)
    from_x(0)
    noise_got(2, h, 1)
    noise_got(1, g, 0)
    from_x(1)
    noise_got(3, h, 0)
    noise_got(1, g, 1)
    noise_got(3, h, 1)
    from_x(2)
    to_x(0)
    noise_got(2, g, 0)
    from_x(3)
    to_x(1)
    noise_got(2, g, 1)
    for i in (2, 3):
        got_data(y_dn, i)
        got_data(y_up, i - 2)

    s_nm[...] = jnp.zeros_like(s_nm)
    s_mn[...] = jnp.zeros_like(s_mn)
    sq_n[...] = jnp.zeros_like(sq_n)
    sq_m[...] = jnp.zeros_like(sq_m)

    def noise_cat(r):
        return jnp.concatenate([noise_f[r * npp + i] for i in range(npp)], axis=1)

    def squares(sq, at, v):
        total = sq[at, :]
        for i in range(v.shape[1] // 128):
            w = v[:, i * 128:(i + 1) * 128].astype(F32)
            total += w * w
        sq[at, :] = total

    def chunk(r, k=None):
        at = pl.ds(0, mb) if k is None else pl.ds(k * half, half)
        a = noise_cat(r)
        d = data_f[r, at, :]
        s_nm[:, at] += lax.dot_general(a, d, NT, preferred_element_type=F32)
        s_mn[at, :] += lax.dot_general(d, a, NT, preferred_element_type=F32)
        squares(sq_m, at, d)
        if k != 1:
            squares(sq_n, pl.ds(0, nb), a)

    def plane(k):
        step = lax.div(k + 1, 2)
        zi = zz(jnp.where(lax.rem(k, 2) == 0, step, -step))
        for hi in (0, 1):
            got_noise(cid(zi, hi, 1 - c), None)

        @pl.when((lax.div(zi, YN) == xl) | (lax.rem(zi, YN) == y))
        def _():
            chunk(zi)

    def near_plane(k, carry):
        plane(k)
        return carry

    lax.fori_loop(0, 3, near_plane, 0)
    noise_got(3, g, 0)
    noise_got(3, g, 1)
    lax.fori_loop(3, 5, near_plane, 0)
    far = zz(4)
    for hi in (0, 1):
        for i in (0, 1):
            got_noise(cid(far, hi, c), i)
        send_noise(cid(far, hi, c), None, c_p)
    lax.fori_loop(5, 8, near_plane, 0)

    def sides(k):
        def body(j, carry):
            r = rid(1, jnp.where(j == 0, 1, 3))
            for i in (2 * k, 2 * k + 1):
                got_data(r, i)
            chunk(r, k)
            return carry

        lax.fori_loop(0, 2, body, 0)

    sides(0)
    for i in range(PARTS):
        got_data(rid(1, 2), i)
    chunk(rid(1, 2))
    sides(1)

    def rows_of(sq):
        t = jnp.sum(jnp.transpose(sq), axis=0, keepdims=True)
        return jnp.concatenate([t[:, k * 128:(k + 1) * 128] for k in range(t.shape[1] // 128)], axis=0)

    ns = rows_of(sq_n[...])
    ds = rows_of(sq_m[...])
    u_col[...] = column(ns)
    v_col[...] = column(ds)
    for k in range(mb // 128):
        at = (slice(None), slice(k * 128, (k + 1) * 128))
        s_nm[at] = (u_col[...] + ds[k:k + 1, :] - 2.0 * s_nm[at]) * scale
    for k in range(nb // 128):
        at = (slice(None), slice(k * 128, (k + 1) * 128))
        s_mn[at] = (v_col[...] + ns[k:k + 1, :] - 2.0 * s_mn[at]) * scale

    col_to = [cid(zz(d), hi, c) for d in (4, 3, -3, 2, -2, 1, -1, 0) for hi in (1 - h, h)][:-1]
    row_to = [rid(dx, dy) for dy in (2, 1, 3, 0) for dx in (1, 0)][:-1]

    def start_core(t):
        cp = remote(core_x.at[t, c], core_x.at[t, c], core_send.at[t], core_recv.at[t], col=c_p)
        cp.start()
        pending.append(cp)

    def start_col(t):
        for to in col_to:
            remote(col_x.at[t, zh], col_x.at[t, zh], col_send.at[t], col_recv.at[t], col=to).start()

    def start_row(t):
        for to in row_to:
            remote(row_x.at[t, row], row_x.at[t, row], row_send.at[t], row_recv.at[t], row=to).start()

    def got_col(t):
        landed(col_x.at[t, pl.ds(0, zh_n - 1)], col_recv.at[t])

    def got_row(t):
        landed(row_x.at[t, pl.ds(0, ROWS - 1)], row_recv.at[t])

    if stage >= 2:
        v_col[...] = jnp.zeros_like(v_col)
        for t in range(ITERS):
            local_lse(s_mn, v_col, core_x.at[t, c])
            start_core(t)
            landed(core_x.at[t, 1 - c], core_recv.at[t])
            col_x[t, zh] = combine(core_x[t])
            start_col(t)
            got_col(t)
            u = -(combine(col_x[t]) + log_rows)
            u_row[...] = u
            u_col[...] = column(u)
            local_lse(s_nm, u_col, row_x.at[t, row])
            start_row(t)
            got_row(t)
            v = -(combine(row_x[t]) + log_cols)
            v_row[...] = v
            v_col[...] = column(v)

    wide = features // KS

    def lanes(r):
        return pl.ds(pl.multiple_of(r * kd, kd), kd)

    if stage >= 3:
        t = ITERS
        logs = log_rows + log_cols
        for k in range(nb // 128):
            at = (slice(None), slice(k * 128, (k + 1) * 128))
            w = jnp.exp2(v_col[...] + u_row[k:k + 1, :] - s_mn[at] + logs).astype(BF16)
            c_mn[at] = w
            core_x[t, c, k:k + 1, :] = jnp.sum(w.astype(F32), axis=0, keepdims=True)
        start_core(t)

        def p_dot(r):
            p_b[r] = lax.dot_general(c_mn[...], noise_cat(r), NN, preferred_element_type=F32).astype(BF16)

        quarter = half // 2

        def p_rows(r, first, count):
            return p_b.at[r, pl.ds(first, count), :]

        leaving = []
        steps = {}

        def leave(src, to, send, recv, **dev):
            remote(src, to[0].at[to[1]], send[0].at[send[1]], recv, **dev).start()
            leaving.append((to, send))

        def lead(k):
            r, dev = ((rid(1, 1), y_up), (rid(1, 3), y_dn), (rid(1, 2), x_p))[k]
            if k < 2:
                for i in (0, 1):
                    leave(p_rows(r, i * half, half), (p_lead, (k, i)), (psend, (k, i)), precv.at[k, i], row=dev)
            else:
                for j in (0, 1):
                    for i in (0, 1):
                        to = (p_lead, (2, i, pl.ds(j * quarter, quarter)))
                        src = p_rows(r, i * half + j * quarter, quarter)
                        leave(src, to, (xqsend, (i, j)), xqrecv.at[i, j], row=dev)

        def coupling():
            for k in range(mb // 128):
                at = (slice(None), slice(k * 128, (k + 1) * 128))
                w = jnp.exp2(u_col[...] + v_row[k:k + 1, :] - s_nm[at] + logs).astype(BF16)
                c_nm[at] = w
                row_x[t, row, k:k + 1, :] = jnp.sum(w.astype(F32), axis=0, keepdims=True)
            start_row(t)

        steps["cnm"] = coupling
        share = nb // cols

        def q_dot(r):
            w = lax.dot_general(c_nm[...], data_f[r], NN, preferred_element_type=F32)
            q_b[:, :, :, lanes(r)] = w.astype(BF16).reshape(zh_n, 2, share, kd)
            remote(q_b.at[:, 1 - c, :, lanes(r)], q_r.at[:, :, lanes(r)],
                   qsend.at[r], qrecv.at[r], col=c_p).start()

        def q_sum(r):
            landed(q_r.at[:, :, lanes(r)], qrecv.at[r])
            q_s[:, :, lanes(r)] = (
                q_b[:, c, :, lanes(r)].astype(F32) + q_r[:, :, lanes(r)].astype(F32)
            ).astype(BF16)

        for r in range(ROWS):
            steps["qs%d" % r] = functools.partial(q_sum, r)

        z_count = [0]

        def z_send(src, dst, sem, dev):
            k = z_count[0]
            z_count[0] += 1
            leave(src, dst, (zsend, k), sem, col=dev)

        def wide_lanes(kk):
            return pl.ds(kk * wide, wide)

        def z_start(kk):
            at = wide_lanes(kk)
            z_send(q_s.at[far * 2, :, at], (z_first, (kk, 0)), zrecv.at[kk, 0, 0], z_up)
            z_send(q_s.at[far * 2 + 1, :, at], (z_first, (kk, 1)), zrecv.at[kk, 0, 1], z_dn)

        def z_add(s, kk, i, zi):
            ln = wide_lanes(kk)
            if s == 1:
                landed(z_first.at[kk, i], zrecv.at[kk, 0, i])
                at = (zi * 2 + i, slice(None), ln)
                q_s[at] = (q_s[at].astype(F32) + z_first[kk, i].astype(F32)).astype(BF16)
            else:
                landed(z_next.at[s - 2, kk, i], zrecv.at[kk, s - 1, i])
                at = (pl.ds(zi * 2, 2), slice(None), ln)
                q_s[at] = (q_s[at].astype(F32) + z_next[s - 2, kk, i].astype(F32)).astype(BF16)

        def z_step(s, kk, i):
            sign, dev = ((1, z_up), (-1, z_dn))[i]
            zi = zz(sign * (4 - s))
            z_add(s, kk, i, zi)
            z_send(q_s.at[pl.ds(zi * 2, 2), :, wide_lanes(kk)], (z_next, (s - 1, kk, i)), zrecv.at[kk, s, i], dev)

        def z_end(kk):
            ln = wide_lanes(kk)
            for i in (0, 1):
                landed(z_next.at[2, kk, i], zrecv.at[kk, 3, i])
            own[:, :, ln] = (
                q_s[pl.ds(z * 2, 2), :, ln].astype(F32)
                + z_next[2, kk, 0].astype(F32) + z_next[2, kk, 1].astype(F32)
            )
            h_out[kk] = own[1 - h, :, ln].astype(BF16)
            z_send(h_out.at[kk], (h_in, kk), hrecv.at[kk], h_p)

        for kk in range(KS):
            steps["z0_%d" % kk] = functools.partial(z_start, kk)
            steps["ze_%d" % kk] = functools.partial(z_end, kk)
            for st in (1, 2, 3):
                for i in (0, 1):
                    steps["z%d_%d_%d" % (st, kk, i)] = functools.partial(z_step, st, kk, i)

        p_count = [0]

        def p_send(src, dst, sem, dev):
            k = p_count[0]
            p_count[0] += 1
            leave(src, dst, (p2send, k), p2recv.at[sem], row=dev)

        def add_to(r, first, count, refs):
            at = (r, pl.ds(first, count), slice(None))
            total = p_b[at].astype(F32)
            for ref in refs:
                total += ref[...].astype(F32)
            p_b[at] = total.astype(BF16)

        def opposite(i, j):
            ref = p_lead.at[2, i, pl.ds(j * quarter, quarter)]
            landed(ref, xqrecv.at[i, j])
            first = i * half + j * quarter
            add_to(across, first, quarter, [ref])
            p_send(p_rows(across, first, quarter), (p_half, (i, j)), 2 * i + j, (y_up, y_dn)[i])

        def over_x(i):
            for k in (0, 1):
                landed(p_lead.at[k, i], precv.at[k, i])
            add_to(x_p, i * half, half, [p_lead.at[0, i], p_lead.at[1, i]])
            p_send(p_rows(x_p, i * half, half), (p_x, i), 4 + i, x_p)

        def beside(i):
            dev = (y_up, y_dn)[i]
            p_send(p_rows(dev, (1 - i) * half, half), (p_next, (i, 1 - i)), 6 + i, dev)

        def beside_sum(i, j):
            dev = (y_up, y_dn)[i]
            landed(p_half.at[i, j], p2recv.at[2 * i + j])
            first = i * half + j * quarter
            add_to(dev, first, quarter, [p_half.at[i, j]])
            p_send(p_rows(dev, first, quarter), (p_next, (i, i, pl.ds(j * quarter, quarter))), 8 + 2 * i + j, dev)

        def send_masses():
            landed(core_x.at[t, 1 - c], core_recv.at[t])
            col_x[t, zh] = core_x[t, 0] + core_x[t, 1]
            start_col(t)

        def masses():
            got_row(t)
            v_col[...] = column(1.0 / jnp.sum(row_x[t], axis=0))
            got_col(t)
            u_col[...] = column(1.0 / jnp.sum(col_x[t], axis=0))

        def noise_out(kk):
            inv = u_col[pl.ds(pl.multiple_of(col * share, share), share), :]
            landed(h_in.at[kk], hrecv.at[kk])
            for k in range(wide // 128):
                at = slice(k * 128, (k + 1) * 128)
                to = slice(kk * wide + k * 128, kk * wide + (k + 1) * 128)
                nt_ref[:, to] = inv * (own[h, :, to] + h_in[kk, :, at].astype(F32))

        def data_out(i):
            at = pl.ds(i * half, half)
            landed(p_x.at[i], p2recv.at[4 + i])
            landed(p_next.at[1 - i, i], p2recv.at[7 - i])
            for j in (0, 1):
                landed(p_next.at[i, i, pl.ds(j * quarter, quarter)], p2recv.at[8 + 2 * i + j])
            for k in range(kd // 128):
                ln = slice(k * 128, (k + 1) * 128)
                dt_ref[at, ln] = v_col[at, :] * (
                    p_b[row, at, ln].astype(F32) + p_x[i, :, ln].astype(F32)
                    + p_next[0, i, :, ln].astype(F32) + p_next[1, i, :, ln].astype(F32)
                )

        steps["massgo"] = send_masses
        steps["mass"] = masses
        for i in (0, 1):
            for j in (0, 1):
                steps["op_%d%d" % (i, j)] = functools.partial(opposite, i, j)
                steps["nb_%d%d" % (i, j)] = functools.partial(beside_sum, i, j)
            steps["ox_%d" % i] = functools.partial(over_x, i)
            steps["na_%d" % i] = functools.partial(beside, i)
            steps["f_%d" % i] = functools.partial(data_out, i)
        for kk in range(KS):
            steps["hf_%d" % kk] = functools.partial(noise_out, kk)

        blocks = dict(lead0=rid(1, 1), lead1=rid(1, 3), lead2=rid(1, 2),
                      Pac=across, Pxp=x_p, Pup=y_up, Pdn=y_dn, Pown=row)
        for k in range(3):
            steps["lead%d" % k] = functools.partial(lead, k)

        def multiply(k, carry):
            r = blocks[MULTIPLIES[0][0]]
            for_noise = k < 0
            for i, (name, *_) in enumerate(MULTIPLIES):
                if name in blocks:
                    r = jnp.where(k == i, blocks[name], r)
                else:
                    r = jnp.where(k == i, int(name[1:]), r)
                    for_noise = for_noise | (k == i)

            @pl.when(for_noise)
            def _():
                q_dot(r)

            @pl.when(jnp.logical_not(for_noise))
            def _():
                p_dot(r)

            for i, (name, *after) in enumerate(MULTIPLIES):
                after = ([name] if name.startswith("lead") else []) + after
                if after:
                    @pl.when(k == i)
                    def _(after=after):
                        for step in after:
                            steps[step]()
            return carry

        lax.fori_loop(0, len(MULTIPLIES), multiply, 0)
        for step in REST:
            steps[step]()
        for r in range(ROWS):
            landed(q_r.at[:, :, lanes(r)], qsend.at[r])
        for to, send in leaving:
            landed(to[0].at[to[1]], send[0].at[send[1]])

    for cp in pending:
        cp.wait_send()
    for t in range(ITERS + 1):
        if (stage >= 2 and t < ITERS) or stage >= 3:
            landed(col_x.at[t, pl.ds(0, zh_n - 1)], col_send.at[t])
            landed(row_x.at[t, pl.ds(0, ROWS - 1)], row_send.at[t])
    if stage < 3:
        nt_ref[...] = jnp.zeros_like(nt_ref)
        dt_ref[...] = s_nm[...] + s_mn[...]


def finish(n_in, d_in, n_out, d_out, sems):
    copies = [pltpu.make_async_copy(n_in, n_out, sems.at[0]), pltpu.make_async_copy(d_in, d_out, sems.at[1])]
    for cp in copies:
        cp.start()
    for cp in copies:
        cp.wait()


def local(noise, data, stage=3, opts=()):
    nb, kn = noise.shape
    mb, kd = data.shape
    cols = 4 * ZN
    zh_n = 2 * ZN
    features = kd * ROWS
    wide = features // KS
    share = nb // cols
    half = mb // 2
    vm = pltpu.VMEM
    dma = pltpu.SemaphoreType.DMA
    ex = ITERS + 1
    scratch = [
        vm(noise.shape, F32), vm(data.shape, F32), dma((1 + PARTS,)),
        vm((cols, nb, kn), BF16), vm((ROWS, mb, kd), BF16),
        vm((nb, mb), F32), vm((mb, nb), F32), vm((nb, mb), BF16), vm((mb, nb), BF16),
        vm((nb, 128), F32), vm((mb, 128), F32), vm((nb, 128), F32), vm((mb, 128), F32),
        vm((nb // 128, 128), F32), vm((mb // 128, 128), F32),
        vm((ex, 2, nb // 128, 128), F32), vm((ex, zh_n, nb // 128, 128), F32), vm((ex, ROWS, mb // 128, 128), F32),
        vm((ROWS, mb, kd), BF16), vm((3, 2, half, kd), BF16), vm((2, 2, half // 2, kd), BF16),
        vm((2, half, kd), BF16), vm((2, 2, half, kd), BF16),
        vm((zh_n, 2, share, features), BF16), vm((zh_n, share, features), BF16), vm((zh_n, share, features), BF16),
        vm((KS, 2, share, wide), BF16), vm((3, KS, 2, 2, share, wide), BF16),
        vm((KS, share, wide), BF16), vm((KS, share, wide), BF16), vm((2, share, features), F32),
        dma((64,)), dma((cols, 2)), dma((28,)), dma((ROWS, PARTS)),
        dma((ex,)), dma((ex,)), dma((ex,)), dma((ex,)), dma((ex,)), dma((ex,)),
        dma((2, 2)), dma((2, 2)), dma((2, 2)), dma((2, 2)), dma((12,)), dma((12,)), dma((ROWS,)), dma((ROWS,)),
        dma((9 * KS,)), dma((KS, 4, 2)), dma((KS,)),
    ]
    sums = pl.pallas_call(
        functools.partial(kernel, (stage, opts)),
        out_shape=(
            pltpu.VMEM((share, features), F32),
            pltpu.VMEM((mb, kd), F32),
        ),
        in_specs=[pl.BlockSpec(memory_space=pltpu.HBM)] * 2,
        out_specs=[pl.BlockSpec(memory_space=pltpu.VMEM)] * 2,
        scratch_shapes=scratch,
        compiler_params=pltpu.CompilerParams(
            collective_id=0, has_side_effects=True, vmem_limit_bytes=125 * 512 * 1024
        ),
    )(noise, data)
    if "nofin" in opts:
        return sums
    return pl.pallas_call(
        finish,
        out_shape=tuple(jax.ShapeDtypeStruct(v.shape, v.dtype) for v in sums),
        in_specs=[pl.BlockSpec(memory_space=pltpu.VMEM)] * 2,
        out_specs=[pl.BlockSpec(memory_space=pl.ANY)] * 2,
        scratch_shapes=[dma((2,))],
        compiler_params=pltpu.CompilerParams(vmem_limit_bytes=8 * 1024 * 1024),
    )(*sums)


def solution(mesh, stage=3, opts=()):
    return jax.shard_map(
        functools.partial(local, stage=stage, opts=opts),
        mesh=mesh,
        in_specs=(P("row", "col"), P("col", "row")),
        out_specs=(P(("row", "col"), None), P("col", "row")),
        check_vma=False,
    )
```

```python
import functools
import math

import jax
import jax.numpy as jnp
from jax import lax
from jax.experimental import pallas as pl
from jax.experimental.pallas import tpu as pltpu
from jax.sharding import PartitionSpec as P

ITERS = 3
YN = 4
ROWS = 8
ZN = 8
PARTS = 4
KS = 4
MULTIPLIES = (
    ("lead0",),
    ("lead1",),
    ("lead2", "cnm"),
    ("q0",),
    ("q1",),
    ("q2",),
    ("q3", "massgo", "qs0"),
    ("q4", "qs1", "z0_0"),
    ("q5", "qs2"),
    ("q6", "qs3", "z0_1"),
    ("q7", "qs4", "z1_0_0", "z1_0_1"),
    ("Pxp", "qs5"),
    ("Pac", "z0_2", "z1_1_1", "z1_1_0", "op_00", "ox_0", "qs7", "qs6", "z0_3", "z2_0_1", "z2_0_0", "op_10"),
    ("Pdn", "z1_2_1", "op_01"),
    ("Pown", "z1_2_0", "z2_1_0", "ox_1", "op_11", "z1_3_1", "z2_1_1"),
    ("Pup",),
)
REST = (
    "na_0", "z1_3_0", "z2_2_0", "z3_0_0", "na_1", "z2_2_1", "z3_0_1", "z3_1_1", "z3_1_0", "nb_01", "z2_3_0",
    "z2_3_1", "z3_2_1", "nb_00", "z3_2_0", "ze_0", "nb_10", "ze_1", "nb_11", "z3_3_0", "z3_3_1", "ze_2",
    "mass", "hf_0", "hf_1", "ze_3", "hf_2", "f_0", "f_1", "hf_3",
)
MESH = pl.DeviceIdType.MESH
F32 = jnp.float32
BF16 = jnp.bfloat16
NT = (((1,), (1,)), ((), ()))
NN = (((1,), (0,)), ((), ()))


def remote(src, dst, send, recv, **dev):
    return pltpu.make_async_remote_copy(
        src_ref=src, dst_ref=dst, send_sem=send, recv_sem=recv,
        device_id=dev, device_id_type=MESH,
    )


def landed(ref, sem):
    pltpu.make_async_copy(ref, ref, sem).wait()


def column(rows4):
    blocks = [
        jnp.transpose(jnp.broadcast_to(rows4[k:k + 1, :], (128, 128)))
        for k in range(rows4.shape[0])
    ]
    return jnp.concatenate(blocks, axis=0)


def local_lse(mat, col, out):
    for k in range(mat.shape[1] // 128):
        x = col[...] - mat[:, k * 128:(k + 1) * 128]
        m = jnp.max(x, axis=0, keepdims=True)
        s = jnp.sum(jnp.exp2(x - m), axis=0, keepdims=True)
        out[k:k + 1, :] = m + jnp.log2(s)


def combine(parts):
    top = jnp.max(parts, axis=0)
    return top + jnp.log2(jnp.sum(jnp.exp2(parts - top[None]), axis=0))


def kernel(
    cfg, noise_hbm, data_hbm, nt_ref, dt_ref, noise_ref, data_ref, in_sem,
    noise_f, data_f, s_nm, s_mn, c_nm, c_mn, u_col, v_col, sq_n, sq_m, u_row, v_row,
    core_x, col_x, row_x,
    p_b, p_lead, p_half, p_x, p_next, q_b, q_r, q_s, z_first, z_next, h_out, h_in, own,
    nsend, nrecv, dsend, drecv,
    core_send, core_recv, col_send, col_recv, row_send, row_recv,
    psend, precv, xqsend, xqrecv, p2send, p2recv, qsend, qrecv, zsend, zrecv, hrecv,
):
    stage, opts = cfg
    zn = ZN
    nb = noise_ref.shape[0]
    mb = data_ref.shape[0]
    kd = data_ref.shape[1]
    kn = noise_ref.shape[1]
    cols = 4 * zn
    npp = cols // ROWS
    zh_n = 2 * zn
    half = mb // 2
    part = mb // PARTS
    fold = nb // 2
    features = kd * ROWS
    scale = math.log2(math.e) / (0.25 * features)
    log_rows = math.log2(nb * ROWS)
    log_cols = math.log2(mb * cols)

    row = lax.axis_index("row")
    col = lax.axis_index("col")
    xl = lax.div(row, YN)
    y = lax.rem(row, YN)
    z = lax.div(col, 4)
    h = lax.rem(lax.div(col, 2), 2)
    c = lax.rem(col, 2)

    def rid(dx, dy):
        return lax.rem(xl + dx, 2) * YN + lax.rem(y + dy, YN)

    def zz(d):
        return lax.rem(z + d + zn, zn)

    def cid(zi, hi, ci):
        return (zi * 2 + hi) * 2 + ci

    y_up, y_dn, x_p = rid(0, 1), rid(0, 3), rid(1, 0)
    z_up, z_dn = cid(zz(1), h, c), cid(zz(-1), h, c)
    h_p = cid(z, 1 - h, c)
    c_p = cid(z, h, 1 - c)
    zh = z * 2 + h

    barrier = pltpu.get_barrier_semaphore()

    def greet(**dev):
        pl.semaphore_signal(barrier, inc=1, device_id=dev, device_id_type=MESH)

    for dev in (y_up, y_dn, x_p):
        greet(row=dev)
    for dev in (z_up, z_dn, h_p, c_p):
        greet(col=dev)
    loads = [pltpu.make_async_copy(noise_hbm, noise_ref, in_sem.at[0])]
    for i in range(PARTS):
        at = pl.ds(i * part, part)
        loads.append(pltpu.make_async_copy(data_hbm.at[at], data_ref.at[at], in_sem.at[1 + i]))
    for cp in loads:
        cp.start()
    loads[0].wait()
    noise_f[col] = noise_ref[...].astype(BF16)
    for i in range(PARTS):
        loads[1 + i].wait()
        data_f[row, i * part:(i + 1) * part, :] = data_ref[i * part:(i + 1) * part, :].astype(BF16)
    pl.semaphore_wait(barrier, 7)

    pending = []
    n_count = [0]
    d_count = [0]

    def noise_part(piece, i):
        return noise_f.at[piece, pl.ds(i * fold, fold), :]

    def send_noise(piece, i, dev):
        k = n_count[0]
        n_count[0] += 1
        ref = noise_f.at[piece] if i is None else noise_part(piece, i)
        cp = remote(ref, ref, nsend.at[k], nrecv.at[piece, 0 if i is None else i], col=dev)
        cp.start()
        pending.append(cp)

    def got_noise(piece, i):
        ref = noise_f.at[piece] if i is None else noise_part(piece, i)
        landed(ref, nrecv.at[piece, 0 if i is None else i])

    def data_part(r, i):
        return data_f.at[r, pl.ds(i * part, part), :]

    def send_data(r, i, dev):
        k = d_count[0]
        d_count[0] += 1
        cp = remote(data_part(r, i), data_part(r, i), dsend.at[k], drecv.at[r, i], row=dev)
        cp.start()
        pending.append(cp)

    def got_data(r, i):
        landed(data_part(r, i), drecv.at[r, i])

    across = rid(0, 2)
    for i in (0, 1):
        send_noise(col, i, h_p)
        send_noise(col, i, z_up)
        send_noise(col, i, z_dn)
        send_data(row, i, y_up)
        send_data(row, i + 2, y_dn)
        send_data(row, i, x_p)
    send_data(row, 2, y_up)
    send_data(row, 0, y_dn)
    send_data(row, 2, x_p)
    send_data(row, 3, x_p)
    send_noise(col, None, c_p)

    def noise_got(s, hi, i):
        up, dn = cid(zz(-s), hi, c), cid(zz(s), hi, c)
        got_noise(up, i)
        if s < 3 or i == 0:
            send_noise(up, i, z_up)
        got_noise(dn, i)
        if s < 3 or i == 1:
            send_noise(dn, i, z_dn)
        if i == 1:
            send_noise(up, None, c_p)
            send_noise(dn, None, c_p)

    def noise_pair(i):
        got_noise(h_p, i)
        send_noise(h_p, i, z_up)
        send_noise(h_p, i, z_dn)
        if i == 1:
            send_noise(h_p, None, c_p)

    def pass_on(i):
        got_data(y_dn, i)
        send_data(y_dn, i, y_up)
        got_data(y_up, i + 2)
        send_data(y_up, i + 2, y_dn)

    def from_x(i):
        got_data(x_p, i)
        send_data(x_p, i, y_up)
        send_data(x_p, i, y_dn)

    def to_x(i):
        for k in (i, i + 2):
            got_data(across, k)
            send_data(across, k, x_p)

    g = 1 - h
    noise_got(1, h, 0)
    noise_pair(0)
    pass_on(0)
    noise_got(1, h, 1)
    noise_pair(1)
    noise_got(2, h, 0)
    pass_on(1)
    send_data(row, 3, y_up)
    send_data(row, 1, y_dn)
    from_x(0)
    noise_got(2, h, 1)
    noise_got(1, g, 0)
    from_x(1)
    noise_got(3, h, 0)
    noise_got(1, g, 1)
    noise_got(3, h, 1)
    from_x(2)
    to_x(0)
    noise_got(2, g, 0)
    from_x(3)
    to_x(1)
    noise_got(2, g, 1)
    for i in (2, 3):
        got_data(y_dn, i)
        got_data(y_up, i - 2)

    s_nm[...] = jnp.zeros_like(s_nm)
    s_mn[...] = jnp.zeros_like(s_mn)
    sq_n[...] = jnp.zeros_like(sq_n)
    sq_m[...] = jnp.zeros_like(sq_m)

    def noise_cat(r):
        return jnp.concatenate([noise_f[r * npp + i] for i in range(npp)], axis=1)

    def squares(sq, at, v):
        total = sq[at, :]
        for i in range(v.shape[1] // 128):
            w = v[:, i * 128:(i + 1) * 128].astype(F32)
            total += w * w
        sq[at, :] = total

    def chunk(r, k=None):
        at = pl.ds(0, mb) if k is None else pl.ds(k * half, half)
        a = noise_cat(r)
        d = data_f[r, at, :]
        s_nm[:, at] += lax.dot_general(a, d, NT, preferred_element_type=F32)
        s_mn[at, :] += lax.dot_general(d, a, NT, preferred_element_type=F32)
        squares(sq_m, at, d)
        if k != 1:
            squares(sq_n, pl.ds(0, nb), a)

    def plane(k):
        step = lax.div(k + 1, 2)
        zi = zz(jnp.where(lax.rem(k, 2) == 0, step, -step))
        for hi in (0, 1):
            got_noise(cid(zi, hi, 1 - c), None)

        @pl.when((lax.div(zi, YN) == xl) | (lax.rem(zi, YN) == y))
        def _():
            chunk(zi)

    def near_plane(k, carry):
        plane(k)
        return carry

    lax.fori_loop(0, 3, near_plane, 0)
    noise_got(3, g, 0)
    noise_got(3, g, 1)
    lax.fori_loop(3, 5, near_plane, 0)
    far = zz(4)
    for hi in (0, 1):
        for i in (0, 1):
            got_noise(cid(far, hi, c), i)
        send_noise(cid(far, hi, c), None, c_p)
    lax.fori_loop(5, 8, near_plane, 0)

    def sides(k):
        def body(j, carry):
            r = rid(1, jnp.where(j == 0, 1, 3))
            for i in (2 * k, 2 * k + 1):
                got_data(r, i)
            chunk(r, k)
            return carry

        lax.fori_loop(0, 2, body, 0)

    def rows_of(sq):
        t = jnp.sum(jnp.transpose(sq), axis=0, keepdims=True)
        return jnp.concatenate([t[:, k * 128:(k + 1) * 128] for k in range(t.shape[1] // 128)], axis=0)

    def scores(i, ns):
        first = i * half
        at = pl.ds(first, half)
        ds = rows_of(sq_m[at, :])
        v_col[at, :] = column(ds)
        for k in range(half // 128):
            ln = (slice(None), pl.ds(first + k * 128, 128))
            s_nm[ln] = (u_col[...] + ds[k:k + 1, :] - 2.0 * s_nm[ln]) * scale
        for k in range(nb // 128):
            ln = (at, slice(k * 128, (k + 1) * 128))
            s_mn[ln] = (v_col[at, :] + ns[k:k + 1, :] - 2.0 * s_mn[ln]) * scale

    sides(0)
    for i in range(PARTS):
        got_data(rid(1, 2), i)
    chunk(rid(1, 2))
    ns = rows_of(sq_n[...])
    u_col[...] = column(ns)
    scores(0, ns)
    sides(1)
    scores(1, ns)


    col_to = [cid(zz(d), hi, c) for d in (4, 3, -3, 2, -2, 1, -1, 0) for hi in (1 - h, h)][:-1]
    row_to = [rid(dx, dy) for dy in (2, 1, 3, 0) for dx in (1, 0)][:-1]

    def start_core(t):
        cp = remote(core_x.at[t, c], core_x.at[t, c], core_send.at[t], core_recv.at[t], col=c_p)
        cp.start()
        pending.append(cp)

    def start_col(t):
        for to in col_to:
            remote(col_x.at[t, zh], col_x.at[t, zh], col_send.at[t], col_recv.at[t], col=to).start()

    def start_row(t):
        for to in row_to:
            remote(row_x.at[t, row], row_x.at[t, row], row_send.at[t], row_recv.at[t], row=to).start()

    def got_col(t):
        landed(col_x.at[t, pl.ds(0, zh_n - 1)], col_recv.at[t])

    def got_row(t):
        landed(row_x.at[t, pl.ds(0, ROWS - 1)], row_recv.at[t])

    if stage >= 2:
        v_col[...] = jnp.zeros_like(v_col)
        for t in range(ITERS):
            local_lse(s_mn, v_col, core_x.at[t, c])
            start_core(t)
            landed(core_x.at[t, 1 - c], core_recv.at[t])
            col_x[t, zh] = combine(core_x[t])
            start_col(t)
            got_col(t)
            u = -(combine(col_x[t]) + log_rows)
            u_row[...] = u
            u_col[...] = column(u)
            local_lse(s_nm, u_col, row_x.at[t, row])
            start_row(t)
            got_row(t)
            v = -(combine(row_x[t]) + log_cols)
            v_row[...] = v
            v_col[...] = column(v)

    wide = features // KS

    def lanes(r):
        return pl.ds(pl.multiple_of(r * kd, kd), kd)

    if stage >= 3:
        t = ITERS
        logs = log_rows + log_cols
        for k in range(nb // 128):
            at = (slice(None), slice(k * 128, (k + 1) * 128))
            w = jnp.exp2(v_col[...] + u_row[k:k + 1, :] - s_mn[at] + logs).astype(BF16)
            c_mn[at] = w
            core_x[t, c, k:k + 1, :] = jnp.sum(w.astype(F32), axis=0, keepdims=True)
        start_core(t)

        def p_dot(r):
            p_b[r] = lax.dot_general(c_mn[...], noise_cat(r), NN, preferred_element_type=F32).astype(BF16)

        quarter = half // 2

        def p_rows(r, first, count):
            return p_b.at[r, pl.ds(first, count), :]

        leaving = []
        steps = {}

        def leave(src, to, send, recv, **dev):
            remote(src, to[0].at[to[1]], send[0].at[send[1]], recv, **dev).start()
            leaving.append((to, send))

        def lead(k):
            r, dev = ((rid(1, 1), y_up), (rid(1, 3), y_dn), (rid(1, 2), x_p))[k]
            if k < 2:
                for i in (0, 1):
                    leave(p_rows(r, i * half, half), (p_lead, (k, i)), (psend, (k, i)), precv.at[k, i], row=dev)
            else:
                for j in (0, 1):
                    for i in (0, 1):
                        to = (p_lead, (2, i, pl.ds(j * quarter, quarter)))
                        src = p_rows(r, i * half + j * quarter, quarter)
                        leave(src, to, (xqsend, (i, j)), xqrecv.at[i, j], row=dev)

        def coupling():
            for k in range(mb // 128):
                at = (slice(None), slice(k * 128, (k + 1) * 128))
                w = jnp.exp2(u_col[...] + v_row[k:k + 1, :] - s_nm[at] + logs).astype(BF16)
                c_nm[at] = w
                row_x[t, row, k:k + 1, :] = jnp.sum(w.astype(F32), axis=0, keepdims=True)
            start_row(t)

        steps["cnm"] = coupling
        share = nb // cols

        def q_dot(r):
            w = lax.dot_general(c_nm[...], data_f[r], NN, preferred_element_type=F32)
            q_b[:, :, :, lanes(r)] = w.astype(BF16).reshape(zh_n, 2, share, kd)
            remote(q_b.at[:, 1 - c, :, lanes(r)], q_r.at[:, :, lanes(r)],
                   qsend.at[r], qrecv.at[r], col=c_p).start()

        def q_sum(r):
            landed(q_r.at[:, :, lanes(r)], qrecv.at[r])
            q_s[:, :, lanes(r)] = (
                q_b[:, c, :, lanes(r)].astype(F32) + q_r[:, :, lanes(r)].astype(F32)
            ).astype(BF16)

        for r in range(ROWS):
            steps["qs%d" % r] = functools.partial(q_sum, r)

        z_count = [0]

        def z_send(src, dst, sem, dev):
            k = z_count[0]
            z_count[0] += 1
            leave(src, dst, (zsend, k), sem, col=dev)

        def wide_lanes(kk):
            return pl.ds(kk * wide, wide)

        def z_start(kk):
            at = wide_lanes(kk)
            z_send(q_s.at[far * 2, :, at], (z_first, (kk, 0)), zrecv.at[kk, 0, 0], z_up)
            z_send(q_s.at[far * 2 + 1, :, at], (z_first, (kk, 1)), zrecv.at[kk, 0, 1], z_dn)

        def z_add(s, kk, i, zi):
            ln = wide_lanes(kk)
            if s == 1:
                landed(z_first.at[kk, i], zrecv.at[kk, 0, i])
                at = (zi * 2 + i, slice(None), ln)
                q_s[at] = (q_s[at].astype(F32) + z_first[kk, i].astype(F32)).astype(BF16)
            else:
                landed(z_next.at[s - 2, kk, i], zrecv.at[kk, s - 1, i])
                at = (pl.ds(zi * 2, 2), slice(None), ln)
                q_s[at] = (q_s[at].astype(F32) + z_next[s - 2, kk, i].astype(F32)).astype(BF16)

        def z_step(s, kk, i):
            sign, dev = ((1, z_up), (-1, z_dn))[i]
            zi = zz(sign * (4 - s))
            z_add(s, kk, i, zi)
            z_send(q_s.at[pl.ds(zi * 2, 2), :, wide_lanes(kk)], (z_next, (s - 1, kk, i)), zrecv.at[kk, s, i], dev)

        def z_end(kk):
            ln = wide_lanes(kk)
            for i in (0, 1):
                landed(z_next.at[2, kk, i], zrecv.at[kk, 3, i])
            own[:, :, ln] = (
                q_s[pl.ds(z * 2, 2), :, ln].astype(F32)
                + z_next[2, kk, 0].astype(F32) + z_next[2, kk, 1].astype(F32)
            )
            h_out[kk] = own[1 - h, :, ln].astype(BF16)
            z_send(h_out.at[kk], (h_in, kk), hrecv.at[kk], h_p)

        for kk in range(KS):
            steps["z0_%d" % kk] = functools.partial(z_start, kk)
            steps["ze_%d" % kk] = functools.partial(z_end, kk)
            for st in (1, 2, 3):
                for i in (0, 1):
                    steps["z%d_%d_%d" % (st, kk, i)] = functools.partial(z_step, st, kk, i)

        p_count = [0]

        def p_send(src, dst, sem, dev):
            k = p_count[0]
            p_count[0] += 1
            leave(src, dst, (p2send, k), p2recv.at[sem], row=dev)

        def add_to(r, first, count, refs):
            at = (r, pl.ds(first, count), slice(None))
            total = p_b[at].astype(F32)
            for ref in refs:
                total += ref[...].astype(F32)
            p_b[at] = total.astype(BF16)

        def opposite(i, j):
            ref = p_lead.at[2, i, pl.ds(j * quarter, quarter)]
            landed(ref, xqrecv.at[i, j])
            first = i * half + j * quarter
            add_to(across, first, quarter, [ref])
            p_send(p_rows(across, first, quarter), (p_half, (i, j)), 2 * i + j, (y_up, y_dn)[i])

        def over_x(i):
            for k in (0, 1):
                landed(p_lead.at[k, i], precv.at[k, i])
            add_to(x_p, i * half, half, [p_lead.at[0, i], p_lead.at[1, i]])
            p_send(p_rows(x_p, i * half, half), (p_x, i), 4 + i, x_p)

        def beside(i):
            dev = (y_up, y_dn)[i]
            p_send(p_rows(dev, (1 - i) * half, half), (p_next, (i, 1 - i)), 6 + i, dev)

        def beside_sum(i, j):
            dev = (y_up, y_dn)[i]
            landed(p_half.at[i, j], p2recv.at[2 * i + j])
            first = i * half + j * quarter
            add_to(dev, first, quarter, [p_half.at[i, j]])
            p_send(p_rows(dev, first, quarter), (p_next, (i, i, pl.ds(j * quarter, quarter))), 8 + 2 * i + j, dev)

        def send_masses():
            landed(core_x.at[t, 1 - c], core_recv.at[t])
            col_x[t, zh] = core_x[t, 0] + core_x[t, 1]
            start_col(t)

        def masses():
            got_row(t)
            v_col[...] = column(1.0 / jnp.sum(row_x[t], axis=0))
            got_col(t)
            u_col[...] = column(1.0 / jnp.sum(col_x[t], axis=0))

        def noise_out(kk):
            inv = u_col[pl.ds(pl.multiple_of(col * share, share), share), :]
            landed(h_in.at[kk], hrecv.at[kk])
            for k in range(wide // 128):
                at = slice(k * 128, (k + 1) * 128)
                to = slice(kk * wide + k * 128, kk * wide + (k + 1) * 128)
                nt_ref[:, to] = inv * (own[h, :, to] + h_in[kk, :, at].astype(F32))

        def data_out(i):
            at = pl.ds(i * half, half)
            landed(p_x.at[i], p2recv.at[4 + i])
            landed(p_next.at[1 - i, i], p2recv.at[7 - i])
            for j in (0, 1):
                landed(p_next.at[i, i, pl.ds(j * quarter, quarter)], p2recv.at[8 + 2 * i + j])
            for k in range(kd // 128):
                ln = slice(k * 128, (k + 1) * 128)
                dt_ref[at, ln] = v_col[at, :] * (
                    p_b[row, at, ln].astype(F32) + p_x[i, :, ln].astype(F32)
                    + p_next[0, i, :, ln].astype(F32) + p_next[1, i, :, ln].astype(F32)
                )

        steps["massgo"] = send_masses
        steps["mass"] = masses
        for i in (0, 1):
            for j in (0, 1):
                steps["op_%d%d" % (i, j)] = functools.partial(opposite, i, j)
                steps["nb_%d%d" % (i, j)] = functools.partial(beside_sum, i, j)
            steps["ox_%d" % i] = functools.partial(over_x, i)
            steps["na_%d" % i] = functools.partial(beside, i)
            steps["f_%d" % i] = functools.partial(data_out, i)
        for kk in range(KS):
            steps["hf_%d" % kk] = functools.partial(noise_out, kk)

        blocks = dict(lead0=rid(1, 1), lead1=rid(1, 3), lead2=rid(1, 2),
                      Pac=across, Pxp=x_p, Pup=y_up, Pdn=y_dn, Pown=row)
        for k in range(3):
            steps["lead%d" % k] = functools.partial(lead, k)

        def multiply(k, carry):
            r = blocks[MULTIPLIES[0][0]]
            for_noise = k < 0
            for i, (name, *_) in enumerate(MULTIPLIES):
                if name in blocks:
                    r = jnp.where(k == i, blocks[name], r)
                else:
                    r = jnp.where(k == i, int(name[1:]), r)
                    for_noise = for_noise | (k == i)

            @pl.when(for_noise)
            def _():
                q_dot(r)

            @pl.when(jnp.logical_not(for_noise))
            def _():
                p_dot(r)

            for i, (name, *after) in enumerate(MULTIPLIES):
                after = ([name] if name.startswith("lead") else []) + after
                if after:
                    @pl.when(k == i)
                    def _(after=after):
                        for step in after:
                            steps[step]()
            return carry

        lax.fori_loop(0, len(MULTIPLIES), multiply, 0)
        for step in REST:
            steps[step]()
        for r in range(ROWS):
            landed(q_r.at[:, :, lanes(r)], qsend.at[r])
        for to, send in leaving:
            landed(to[0].at[to[1]], send[0].at[send[1]])

    for cp in pending:
        cp.wait_send()
    for t in range(ITERS + 1):
        if (stage >= 2 and t < ITERS) or stage >= 3:
            landed(col_x.at[t, pl.ds(0, zh_n - 1)], col_send.at[t])
            landed(row_x.at[t, pl.ds(0, ROWS - 1)], row_send.at[t])
    if stage < 3:
        nt_ref[...] = jnp.zeros_like(nt_ref)
        dt_ref[...] = s_nm[...] + s_mn[...]


def finish(n_in, d_in, n_out, d_out, sems):
    copies = [pltpu.make_async_copy(n_in, n_out, sems.at[0]), pltpu.make_async_copy(d_in, d_out, sems.at[1])]
    for cp in copies:
        cp.start()
    for cp in copies:
        cp.wait()


def local(noise, data, stage=3, opts=()):
    nb, kn = noise.shape
    mb, kd = data.shape
    cols = 4 * ZN
    zh_n = 2 * ZN
    features = kd * ROWS
    wide = features // KS
    share = nb // cols
    half = mb // 2
    vm = pltpu.VMEM
    dma = pltpu.SemaphoreType.DMA
    ex = ITERS + 1
    scratch = [
        vm(noise.shape, F32), vm(data.shape, F32), dma((1 + PARTS,)),
        vm((cols, nb, kn), BF16), vm((ROWS, mb, kd), BF16),
        vm((nb, mb), F32), vm((mb, nb), F32), vm((nb, mb), BF16), vm((mb, nb), BF16),
        vm((nb, 128), F32), vm((mb, 128), F32), vm((nb, 128), F32), vm((mb, 128), F32),
        vm((nb // 128, 128), F32), vm((mb // 128, 128), F32),
        vm((ex, 2, nb // 128, 128), F32), vm((ex, zh_n, nb // 128, 128), F32), vm((ex, ROWS, mb // 128, 128), F32),
        vm((ROWS, mb, kd), BF16), vm((3, 2, half, kd), BF16), vm((2, 2, half // 2, kd), BF16),
        vm((2, half, kd), BF16), vm((2, 2, half, kd), BF16),
        vm((zh_n, 2, share, features), BF16), vm((zh_n, share, features), BF16), vm((zh_n, share, features), BF16),
        vm((KS, 2, share, wide), BF16), vm((3, KS, 2, 2, share, wide), BF16),
        vm((KS, share, wide), BF16), vm((KS, share, wide), BF16), vm((2, share, features), F32),
        dma((64,)), dma((cols, 2)), dma((28,)), dma((ROWS, PARTS)),
        dma((ex,)), dma((ex,)), dma((ex,)), dma((ex,)), dma((ex,)), dma((ex,)),
        dma((2, 2)), dma((2, 2)), dma((2, 2)), dma((2, 2)), dma((12,)), dma((12,)), dma((ROWS,)), dma((ROWS,)),
        dma((9 * KS,)), dma((KS, 4, 2)), dma((KS,)),
    ]
    sums = pl.pallas_call(
        functools.partial(kernel, (stage, opts)),
        out_shape=(
            pltpu.VMEM((share, features), F32),
            pltpu.VMEM((mb, kd), F32),
        ),
        in_specs=[pl.BlockSpec(memory_space=pltpu.HBM)] * 2,
        out_specs=[pl.BlockSpec(memory_space=pltpu.VMEM)] * 2,
        scratch_shapes=scratch,
        compiler_params=pltpu.CompilerParams(
            collective_id=0, has_side_effects=True, vmem_limit_bytes=125 * 512 * 1024
        ),
    )(noise, data)
    if "nofin" in opts:
        return sums
    return pl.pallas_call(
        finish,
        out_shape=tuple(jax.ShapeDtypeStruct(v.shape, v.dtype) for v in sums),
        in_specs=[pl.BlockSpec(memory_space=pltpu.VMEM)] * 2,
        out_specs=[pl.BlockSpec(memory_space=pl.ANY)] * 2,
        scratch_shapes=[dma((2,))],
        compiler_params=pltpu.CompilerParams(vmem_limit_bytes=8 * 1024 * 1024),
    )(*sums)


def solution(mesh, stage=3, opts=()):
    return jax.shard_map(
        functools.partial(local, stage=stage, opts=opts),
        mesh=mesh,
        in_specs=(P("row", "col"), P("col", "row")),
        out_specs=(P(("row", "col"), None), P("col", "row")),
        check_vma=False,
    )
```

```python
import functools
import math

import jax
import jax.numpy as jnp
from jax import lax
from jax.experimental import pallas as pl
from jax.experimental.pallas import tpu as pltpu
from jax.sharding import PartitionSpec as P

ITERS = 3
YN = 4
ROWS = 8
ZN = 8
PARTS = 4
KS = 4
MULTIPLIES = (
    ("lead0",),
    ("lead1", "cnm"),
    ("q0",),
    ("lead2",),
    ("q1",),
    ("q3", "qs0"),
    ("q2", "massgo", "qs1", "z0_0"),
    ("q4",),
    ("q6", "qs3", "qs2", "z0_1"),
    ("q5",),
    ("q7", "z1_0_0", "z1_0_1", "qs4", "qs5", "z0_2"),
    ("Pac", "qs6", "op_00", "qs7", "z0_3", "z1_1_1", "z1_1_0"),
    ("Pxp", "op_10", "ox_0", "z2_0_1", "z2_0_0", "z1_2_1", "z1_2_0"),
    ("Pdn", "op_01", "z1_3_0"),
    ("Pup", "na_0", "z2_1_0", "z1_3_1", "z3_0_0", "op_11", "z2_1_1", "z2_2_0", "ox_1", "z2_2_1", "na_1", "z3_0_1", "nb_01", "nb_00", "z3_1_1", "z2_3_1", "z3_1_0", "z2_3_0", "z3_2_1", "z3_2_0", "ze_0", "nb_10", "ze_1", "nb_11", "z3_3_0", "z3_3_1"),
    ("Pown",),
)
REST = (
    "ze_2", "mass", "ze_3", "f_0", "hf_1", "hf_0", "hf_2", "f_1", "hf_3",
)
MESH = pl.DeviceIdType.MESH
F32 = jnp.float32
BF16 = jnp.bfloat16
NT = (((1,), (1,)), ((), ()))
NN = (((1,), (0,)), ((), ()))


def remote(src, dst, send, recv, **dev):
    return pltpu.make_async_remote_copy(
        src_ref=src, dst_ref=dst, send_sem=send, recv_sem=recv,
        device_id=dev, device_id_type=MESH,
    )


def landed(ref, sem):
    pltpu.make_async_copy(ref, ref, sem).wait()


def column(rows4):
    blocks = [
        jnp.transpose(jnp.broadcast_to(rows4[k:k + 1, :], (128, 128)))
        for k in range(rows4.shape[0])
    ]
    return jnp.concatenate(blocks, axis=0)


def local_lse(mat, col, out):
    for k in range(mat.shape[1] // 128):
        x = col[...] - mat[:, k * 128:(k + 1) * 128]
        m = jnp.max(x, axis=0, keepdims=True)
        s = jnp.sum(jnp.exp2(x - m), axis=0, keepdims=True)
        out[k:k + 1, :] = m + jnp.log2(s)


def combine(parts):
    top = jnp.max(parts, axis=0)
    return top + jnp.log2(jnp.sum(jnp.exp2(parts - top[None]), axis=0))


def kernel(
    cfg, noise_hbm, data_hbm, nt_ref, dt_ref, noise_ref, data_ref, in_sem,
    noise_f, data_f, s_nm, s_mn, c_nm, c_mn, u_col, v_col, sq_n, sq_m, u_row, v_row,
    core_x, col_x, row_x,
    p_b, p_lead, p_half, p_x, p_next, q_b, q_r, q_s, z_first, z_next, h_out, h_in, own,
    nsend, nrecv, dsend, drecv,
    core_send, core_recv, col_send, col_recv, row_send, row_recv,
    psend, precv, xqsend, xqrecv, p2send, p2recv, qsend, qrecv, zsend, zrecv, hrecv,
):
    stage, opts = cfg
    zn = ZN
    nb = noise_ref.shape[0]
    mb = data_ref.shape[0]
    kd = data_ref.shape[1]
    kn = noise_ref.shape[1]
    cols = 4 * zn
    npp = cols // ROWS
    zh_n = 2 * zn
    half = mb // 2
    part = mb // PARTS
    fold = nb // 2
    features = kd * ROWS
    scale = math.log2(math.e) / (0.25 * features)
    log_rows = math.log2(nb * ROWS)
    log_cols = math.log2(mb * cols)

    row = lax.axis_index("row")
    col = lax.axis_index("col")
    xl = lax.div(row, YN)
    y = lax.rem(row, YN)
    z = lax.div(col, 4)
    h = lax.rem(lax.div(col, 2), 2)
    c = lax.rem(col, 2)

    def rid(dx, dy):
        return lax.rem(xl + dx, 2) * YN + lax.rem(y + dy, YN)

    def zz(d):
        return lax.rem(z + d + zn, zn)

    def cid(zi, hi, ci):
        return (zi * 2 + hi) * 2 + ci

    y_up, y_dn, x_p = rid(0, 1), rid(0, 3), rid(1, 0)
    z_up, z_dn = cid(zz(1), h, c), cid(zz(-1), h, c)
    h_p = cid(z, 1 - h, c)
    c_p = cid(z, h, 1 - c)
    zh = z * 2 + h

    barrier = pltpu.get_barrier_semaphore()

    def greet(**dev):
        pl.semaphore_signal(barrier, inc=1, device_id=dev, device_id_type=MESH)

    for dev in (y_up, y_dn, x_p):
        greet(row=dev)
    for dev in (z_up, z_dn, h_p, c_p):
        greet(col=dev)
    loads = [pltpu.make_async_copy(noise_hbm, noise_ref, in_sem.at[0])]
    for i in range(PARTS):
        at = pl.ds(i * part, part)
        loads.append(pltpu.make_async_copy(data_hbm.at[at], data_ref.at[at], in_sem.at[1 + i]))
    for cp in loads:
        cp.start()
    loads[0].wait()
    noise_f[col] = noise_ref[...].astype(BF16)
    for i in range(PARTS):
        loads[1 + i].wait()
        data_f[row, i * part:(i + 1) * part, :] = data_ref[i * part:(i + 1) * part, :].astype(BF16)
    pl.semaphore_wait(barrier, 7)

    pending = []
    n_count = [0]
    d_count = [0]

    def noise_part(piece, i):
        return noise_f.at[piece, pl.ds(i * fold, fold), :]

    def send_noise(piece, i, dev):
        k = n_count[0]
        n_count[0] += 1
        ref = noise_f.at[piece] if i is None else noise_part(piece, i)
        cp = remote(ref, ref, nsend.at[k], nrecv.at[piece, 0 if i is None else i], col=dev)
        cp.start()
        pending.append(cp)

    def got_noise(piece, i):
        ref = noise_f.at[piece] if i is None else noise_part(piece, i)
        landed(ref, nrecv.at[piece, 0 if i is None else i])

    def data_part(r, i):
        return data_f.at[r, pl.ds(i * part, part), :]

    def send_data(r, i, dev):
        k = d_count[0]
        d_count[0] += 1
        cp = remote(data_part(r, i), data_part(r, i), dsend.at[k], drecv.at[r, i], row=dev)
        cp.start()
        pending.append(cp)

    def got_data(r, i):
        landed(data_part(r, i), drecv.at[r, i])

    across = rid(0, 2)
    for i in (0, 1):
        send_noise(col, i, h_p)
        send_noise(col, i, z_up)
        send_noise(col, i, z_dn)
        send_data(row, i, y_up)
        send_data(row, i + 2, y_dn)
        send_data(row, i, x_p)
    send_data(row, 2, y_up)
    send_data(row, 0, y_dn)
    send_data(row, 2, x_p)
    send_data(row, 3, x_p)
    send_noise(col, None, c_p)

    def noise_got(s, hi, i):
        up, dn = cid(zz(-s), hi, c), cid(zz(s), hi, c)
        got_noise(up, i)
        if s < 3 or i == 0:
            send_noise(up, i, z_up)
        got_noise(dn, i)
        if s < 3 or i == 1:
            send_noise(dn, i, z_dn)
        if i == 1:
            send_noise(up, None, c_p)
            send_noise(dn, None, c_p)

    def noise_pair(i):
        got_noise(h_p, i)
        send_noise(h_p, i, z_up)
        send_noise(h_p, i, z_dn)
        if i == 1:
            send_noise(h_p, None, c_p)

    def pass_on(i):
        got_data(y_dn, i)
        send_data(y_dn, i, y_up)
        got_data(y_up, i + 2)
        send_data(y_up, i + 2, y_dn)

    def from_x(i):
        got_data(x_p, i)
        send_data(x_p, i, y_up)
        send_data(x_p, i, y_dn)

    def to_x(i):
        for k in (i, i + 2):
            got_data(across, k)
            send_data(across, k, x_p)

    g = 1 - h
    noise_got(1, h, 0)
    noise_pair(0)
    pass_on(0)
    noise_got(1, h, 1)
    noise_pair(1)
    noise_got(2, h, 0)
    pass_on(1)
    send_data(row, 3, y_up)
    send_data(row, 1, y_dn)
    from_x(0)
    noise_got(2, h, 1)
    noise_got(1, g, 0)
    from_x(1)
    noise_got(3, h, 0)
    noise_got(1, g, 1)
    noise_got(3, h, 1)
    from_x(2)
    to_x(0)
    noise_got(2, g, 0)
    from_x(3)
    to_x(1)
    noise_got(2, g, 1)
    for i in (2, 3):
        got_data(y_dn, i)
        got_data(y_up, i - 2)

    s_nm[...] = jnp.zeros_like(s_nm)
    s_mn[...] = jnp.zeros_like(s_mn)
    sq_n[...] = jnp.zeros_like(sq_n)
    sq_m[...] = jnp.zeros_like(sq_m)

    def noise_cat(r):
        return jnp.concatenate([noise_f[r * npp + i] for i in range(npp)], axis=1)

    def squares(sq, at, v):
        total = sq[at, :]
        for i in range(v.shape[1] // 128):
            w = v[:, i * 128:(i + 1) * 128].astype(F32)
            total += w * w
        sq[at, :] = total

    def chunk(r, k=None):
        at = pl.ds(0, mb) if k is None else pl.ds(k * half, half)
        a = noise_cat(r)
        d = data_f[r, at, :]
        s_nm[:, at] += lax.dot_general(a, d, NT, preferred_element_type=F32)
        s_mn[at, :] += lax.dot_general(d, a, NT, preferred_element_type=F32)
        squares(sq_m, at, d)
        if k != 1:
            squares(sq_n, pl.ds(0, nb), a)

    def plane(k):
        step = lax.div(k + 1, 2)
        zi = zz(jnp.where(lax.rem(k, 2) == 0, step, -step))
        for hi in (0, 1):
            got_noise(cid(zi, hi, 1 - c), None)

        @pl.when((lax.div(zi, YN) == xl) | (lax.rem(zi, YN) == y))
        def _():
            chunk(zi)

    def near_plane(k, carry):
        plane(k)
        return carry

    lax.fori_loop(0, 3, near_plane, 0)
    noise_got(3, g, 0)
    noise_got(3, g, 1)
    lax.fori_loop(3, 5, near_plane, 0)
    far = zz(4)
    for hi in (0, 1):
        for i in (0, 1):
            got_noise(cid(far, hi, c), i)
        send_noise(cid(far, hi, c), None, c_p)
    lax.fori_loop(5, 8, near_plane, 0)

    def sides(k):
        def body(j, carry):
            r = rid(1, jnp.where(j == 0, 1, 3))
            for i in (2 * k, 2 * k + 1):
                got_data(r, i)
            chunk(r, k)
            return carry

        lax.fori_loop(0, 2, body, 0)

    sides(0)
    for i in range(PARTS):
        got_data(rid(1, 2), i)
    chunk(rid(1, 2))
    sides(1)

    def rows_of(sq):
        t = jnp.sum(jnp.transpose(sq), axis=0, keepdims=True)
        return jnp.concatenate([t[:, k * 128:(k + 1) * 128] for k in range(t.shape[1] // 128)], axis=0)

    ns = rows_of(sq_n[...])
    ds = rows_of(sq_m[...])
    u_col[...] = column(ns)
    v_col[...] = column(ds)
    for k in range(mb // 128):
        at = (slice(None), slice(k * 128, (k + 1) * 128))
        s_nm[at] = (u_col[...] + ds[k:k + 1, :] - 2.0 * s_nm[at]) * scale
    for k in range(nb // 128):
        at = (slice(None), slice(k * 128, (k + 1) * 128))
        s_mn[at] = (v_col[...] + ns[k:k + 1, :] - 2.0 * s_mn[at]) * scale

    col_to = [cid(zz(d), hi, c) for d in (4, 3, -3, 2, -2, 1, -1, 0) for hi in (1 - h, h)][:-1]
    row_to = [rid(dx, dy) for dy in (2, 1, 3, 0) for dx in (1, 0)][:-1]

    def start_core(t):
        cp = remote(core_x.at[t, c], core_x.at[t, c], core_send.at[t], core_recv.at[t], col=c_p)
        cp.start()
        pending.append(cp)

    def start_col(t):
        for to in col_to:
            remote(col_x.at[t, zh], col_x.at[t, zh], col_send.at[t], col_recv.at[t], col=to).start()

    def start_row(t):
        for to in row_to:
            remote(row_x.at[t, row], row_x.at[t, row], row_send.at[t], row_recv.at[t], row=to).start()

    def got_col(t):
        landed(col_x.at[t, pl.ds(0, zh_n - 1)], col_recv.at[t])

    def got_row(t):
        landed(row_x.at[t, pl.ds(0, ROWS - 1)], row_recv.at[t])

    if stage >= 2:
        v_col[...] = jnp.zeros_like(v_col)
        for t in range(ITERS):
            local_lse(s_mn, v_col, core_x.at[t, c])
            start_core(t)
            landed(core_x.at[t, 1 - c], core_recv.at[t])
            col_x[t, zh] = combine(core_x[t])
            start_col(t)
            got_col(t)
            u = -(combine(col_x[t]) + log_rows)
            u_row[...] = u
            u_col[...] = column(u)
            local_lse(s_nm, u_col, row_x.at[t, row])
            start_row(t)
            got_row(t)
            v = -(combine(row_x[t]) + log_cols)
            v_row[...] = v
            v_col[...] = column(v)

    wide = features // KS

    def lanes(r):
        return pl.ds(pl.multiple_of(r * kd, kd), kd)

    if stage >= 3:
        t = ITERS
        logs = log_rows + log_cols
        for k in range(nb // 128):
            at = (slice(None), slice(k * 128, (k + 1) * 128))
            w = jnp.exp2(v_col[...] + u_row[k:k + 1, :] - s_mn[at] + logs).astype(BF16)
            c_mn[at] = w
            core_x[t, c, k:k + 1, :] = jnp.sum(w.astype(F32), axis=0, keepdims=True)
        start_core(t)

        def p_dot(r):
            p_b[r] = lax.dot_general(c_mn[...], noise_cat(r), NN, preferred_element_type=F32).astype(BF16)

        quarter = half // 2

        def p_rows(r, first, count):
            return p_b.at[r, pl.ds(first, count), :]

        leaving = []
        steps = {}

        def leave(src, to, send, recv, **dev):
            remote(src, to[0].at[to[1]], send[0].at[send[1]], recv, **dev).start()
            leaving.append((to, send))

        def lead(k):
            r, dev = ((rid(1, 1), y_up), (rid(1, 3), y_dn), (rid(1, 2), x_p))[k]
            if k < 2:
                for i in (0, 1):
                    leave(p_rows(r, i * half, half), (p_lead, (k, i)), (psend, (k, i)), precv.at[k, i], row=dev)
            else:
                for j in (0, 1):
                    for i in (0, 1):
                        to = (p_lead, (2, i, pl.ds(j * quarter, quarter)))
                        src = p_rows(r, i * half + j * quarter, quarter)
                        leave(src, to, (xqsend, (i, j)), xqrecv.at[i, j], row=dev)

        def coupling():
            for k in range(mb // 128):
                at = (slice(None), slice(k * 128, (k + 1) * 128))
                w = jnp.exp2(u_col[...] + v_row[k:k + 1, :] - s_nm[at] + logs).astype(BF16)
                c_nm[at] = w
                row_x[t, row, k:k + 1, :] = jnp.sum(w.astype(F32), axis=0, keepdims=True)
            start_row(t)

        steps["cnm"] = coupling
        share = nb // cols

        def q_dot(r):
            w = lax.dot_general(c_nm[...], data_f[r], NN, preferred_element_type=F32)
            q_b[:, :, :, lanes(r)] = w.astype(BF16).reshape(zh_n, 2, share, kd)
            remote(q_b.at[:, 1 - c, :, lanes(r)], q_r.at[:, :, lanes(r)],
                   qsend.at[r], qrecv.at[r], col=c_p).start()

        def q_sum(r):
            landed(q_r.at[:, :, lanes(r)], qrecv.at[r])
            q_s[:, :, lanes(r)] = (
                q_b[:, c, :, lanes(r)].astype(F32) + q_r[:, :, lanes(r)].astype(F32)
            ).astype(BF16)

        for r in range(ROWS):
            steps["qs%d" % r] = functools.partial(q_sum, r)

        z_count = [0]

        def z_send(src, dst, sem, dev):
            k = z_count[0]
            z_count[0] += 1
            leave(src, dst, (zsend, k), sem, col=dev)

        def wide_lanes(kk):
            return pl.ds(kk * wide, wide)

        def z_start(kk):
            at = wide_lanes(kk)
            z_send(q_s.at[far * 2, :, at], (z_first, (kk, 0)), zrecv.at[kk, 0, 0], z_up)
            z_send(q_s.at[far * 2 + 1, :, at], (z_first, (kk, 1)), zrecv.at[kk, 0, 1], z_dn)

        def z_add(s, kk, i, zi):
            ln = wide_lanes(kk)
            if s == 1:
                landed(z_first.at[kk, i], zrecv.at[kk, 0, i])
                at = (zi * 2 + i, slice(None), ln)
                q_s[at] = (q_s[at].astype(F32) + z_first[kk, i].astype(F32)).astype(BF16)
            else:
                landed(z_next.at[s - 2, kk, i], zrecv.at[kk, s - 1, i])
                at = (pl.ds(zi * 2, 2), slice(None), ln)
                q_s[at] = (q_s[at].astype(F32) + z_next[s - 2, kk, i].astype(F32)).astype(BF16)

        def z_step(s, kk, i):
            sign, dev = ((1, z_up), (-1, z_dn))[i]
            zi = zz(sign * (4 - s))
            z_add(s, kk, i, zi)
            z_send(q_s.at[pl.ds(zi * 2, 2), :, wide_lanes(kk)], (z_next, (s - 1, kk, i)), zrecv.at[kk, s, i], dev)

        def z_end(kk):
            ln = wide_lanes(kk)
            for i in (0, 1):
                landed(z_next.at[2, kk, i], zrecv.at[kk, 3, i])
            own[:, :, ln] = (
                q_s[pl.ds(z * 2, 2), :, ln].astype(F32)
                + z_next[2, kk, 0].astype(F32) + z_next[2, kk, 1].astype(F32)
            )
            h_out[kk] = own[1 - h, :, ln].astype(BF16)
            z_send(h_out.at[kk], (h_in, kk), hrecv.at[kk], h_p)

        for kk in range(KS):
            steps["z0_%d" % kk] = functools.partial(z_start, kk)
            steps["ze_%d" % kk] = functools.partial(z_end, kk)
            for st in (1, 2, 3):
                for i in (0, 1):
                    steps["z%d_%d_%d" % (st, kk, i)] = functools.partial(z_step, st, kk, i)

        p_count = [0]

        def p_send(src, dst, sem, dev):
            k = p_count[0]
            p_count[0] += 1
            leave(src, dst, (p2send, k), p2recv.at[sem], row=dev)

        def add_to(r, first, count, refs):
            at = (r, pl.ds(first, count), slice(None))
            total = p_b[at].astype(F32)
            for ref in refs:
                total += ref[...].astype(F32)
            p_b[at] = total.astype(BF16)

        def opposite(i, j):
            ref = p_lead.at[2, i, pl.ds(j * quarter, quarter)]
            landed(ref, xqrecv.at[i, j])
            first = i * half + j * quarter
            add_to(across, first, quarter, [ref])
            p_send(p_rows(across, first, quarter), (p_half, (i, j)), 2 * i + j, (y_up, y_dn)[i])

        def over_x(i):
            for k in (0, 1):
                landed(p_lead.at[k, i], precv.at[k, i])
            add_to(x_p, i * half, half, [p_lead.at[0, i], p_lead.at[1, i]])
            p_send(p_rows(x_p, i * half, half), (p_x, i), 4 + i, x_p)

        def beside(i):
            dev = (y_up, y_dn)[i]
            p_send(p_rows(dev, (1 - i) * half, half), (p_next, (i, 1 - i)), 6 + i, dev)

        def beside_sum(i, j):
            dev = (y_up, y_dn)[i]
            landed(p_half.at[i, j], p2recv.at[2 * i + j])
            first = i * half + j * quarter
            add_to(dev, first, quarter, [p_half.at[i, j]])
            p_send(p_rows(dev, first, quarter), (p_next, (i, i, pl.ds(j * quarter, quarter))), 8 + 2 * i + j, dev)

        def send_masses():
            landed(core_x.at[t, 1 - c], core_recv.at[t])
            col_x[t, zh] = core_x[t, 0] + core_x[t, 1]
            start_col(t)

        def masses():
            got_row(t)
            v_col[...] = column(1.0 / jnp.sum(row_x[t], axis=0))
            got_col(t)
            u_col[...] = column(1.0 / jnp.sum(col_x[t], axis=0))

        def noise_out(kk):
            inv = u_col[pl.ds(pl.multiple_of(col * share, share), share), :]
            landed(h_in.at[kk], hrecv.at[kk])
            for k in range(wide // 128):
                at = slice(k * 128, (k + 1) * 128)
                to = slice(kk * wide + k * 128, kk * wide + (k + 1) * 128)
                nt_ref[:, to] = inv * (own[h, :, to] + h_in[kk, :, at].astype(F32))

        def data_out(i):
            at = pl.ds(i * half, half)
            landed(p_x.at[i], p2recv.at[4 + i])
            landed(p_next.at[1 - i, i], p2recv.at[7 - i])
            for j in (0, 1):
                landed(p_next.at[i, i, pl.ds(j * quarter, quarter)], p2recv.at[8 + 2 * i + j])
            for k in range(kd // 128):
                ln = slice(k * 128, (k + 1) * 128)
                dt_ref[at, ln] = v_col[at, :] * (
                    p_b[row, at, ln].astype(F32) + p_x[i, :, ln].astype(F32)
                    + p_next[0, i, :, ln].astype(F32) + p_next[1, i, :, ln].astype(F32)
                )

        steps["massgo"] = send_masses
        steps["mass"] = masses
        for i in (0, 1):
            for j in (0, 1):
                steps["op_%d%d" % (i, j)] = functools.partial(opposite, i, j)
                steps["nb_%d%d" % (i, j)] = functools.partial(beside_sum, i, j)
            steps["ox_%d" % i] = functools.partial(over_x, i)
            steps["na_%d" % i] = functools.partial(beside, i)
            steps["f_%d" % i] = functools.partial(data_out, i)
        for kk in range(KS):
            steps["hf_%d" % kk] = functools.partial(noise_out, kk)

        blocks = dict(lead0=rid(1, 1), lead1=rid(1, 3), lead2=rid(1, 2),
                      Pac=across, Pxp=x_p, Pup=y_up, Pdn=y_dn, Pown=row)
        for k in range(3):
            steps["lead%d" % k] = functools.partial(lead, k)

        def multiply(k, carry):
            r = blocks[MULTIPLIES[0][0]]
            for_noise = k < 0
            for i, (name, *_) in enumerate(MULTIPLIES):
                if name in blocks:
                    r = jnp.where(k == i, blocks[name], r)
                else:
                    r = jnp.where(k == i, int(name[1:]), r)
                    for_noise = for_noise | (k == i)

            @pl.when(for_noise)
            def _():
                q_dot(r)

            @pl.when(jnp.logical_not(for_noise))
            def _():
                p_dot(r)

            for i, (name, *after) in enumerate(MULTIPLIES):
                after = ([name] if name.startswith("lead") else []) + after
                if after:
                    @pl.when(k == i)
                    def _(after=after):
                        for step in after:
                            steps[step]()
            return carry

        lax.fori_loop(0, len(MULTIPLIES), multiply, 0)
        for step in REST:
            steps[step]()
        for r in range(ROWS):
            landed(q_r.at[:, :, lanes(r)], qsend.at[r])
        for to, send in leaving:
            landed(to[0].at[to[1]], send[0].at[send[1]])

    for cp in pending:
        cp.wait_send()
    for t in range(ITERS + 1):
        if (stage >= 2 and t < ITERS) or stage >= 3:
            landed(col_x.at[t, pl.ds(0, zh_n - 1)], col_send.at[t])
            landed(row_x.at[t, pl.ds(0, ROWS - 1)], row_send.at[t])
    if stage < 3:
        nt_ref[...] = jnp.zeros_like(nt_ref)
        dt_ref[...] = s_nm[...] + s_mn[...]


def finish(n_in, d_in, n_out, d_out, sems):
    copies = [pltpu.make_async_copy(n_in, n_out, sems.at[0]), pltpu.make_async_copy(d_in, d_out, sems.at[1])]
    for cp in copies:
        cp.start()
    for cp in copies:
        cp.wait()


def local(noise, data, stage=3, opts=()):
    nb, kn = noise.shape
    mb, kd = data.shape
    cols = 4 * ZN
    zh_n = 2 * ZN
    features = kd * ROWS
    wide = features // KS
    share = nb // cols
    half = mb // 2
    vm = pltpu.VMEM
    dma = pltpu.SemaphoreType.DMA
    ex = ITERS + 1
    scratch = [
        vm(noise.shape, F32), vm(data.shape, F32), dma((1 + PARTS,)),
        vm((cols, nb, kn), BF16), vm((ROWS, mb, kd), BF16),
        vm((nb, mb), F32), vm((mb, nb), F32), vm((nb, mb), BF16), vm((mb, nb), BF16),
        vm((nb, 128), F32), vm((mb, 128), F32), vm((nb, 128), F32), vm((mb, 128), F32),
        vm((nb // 128, 128), F32), vm((mb // 128, 128), F32),
        vm((ex, 2, nb // 128, 128), F32), vm((ex, zh_n, nb // 128, 128), F32), vm((ex, ROWS, mb // 128, 128), F32),
        vm((ROWS, mb, kd), BF16), vm((3, 2, half, kd), BF16), vm((2, 2, half // 2, kd), BF16),
        vm((2, half, kd), BF16), vm((2, 2, half, kd), BF16),
        vm((zh_n, 2, share, features), BF16), vm((zh_n, share, features), BF16), vm((zh_n, share, features), BF16),
        vm((KS, 2, share, wide), BF16), vm((3, KS, 2, 2, share, wide), BF16),
        vm((KS, share, wide), BF16), vm((KS, share, wide), BF16), vm((2, share, features), F32),
        dma((64,)), dma((cols, 2)), dma((28,)), dma((ROWS, PARTS)),
        dma((ex,)), dma((ex,)), dma((ex,)), dma((ex,)), dma((ex,)), dma((ex,)),
        dma((2, 2)), dma((2, 2)), dma((2, 2)), dma((2, 2)), dma((12,)), dma((12,)), dma((ROWS,)), dma((ROWS,)),
        dma((9 * KS,)), dma((KS, 4, 2)), dma((KS,)),
    ]
    sums = pl.pallas_call(
        functools.partial(kernel, (stage, opts)),
        out_shape=(
            pltpu.VMEM((share, features), F32),
            pltpu.VMEM((mb, kd), F32),
        ),
        in_specs=[pl.BlockSpec(memory_space=pltpu.HBM)] * 2,
        out_specs=[pl.BlockSpec(memory_space=pltpu.VMEM)] * 2,
        scratch_shapes=scratch,
        compiler_params=pltpu.CompilerParams(
            collective_id=0, has_side_effects=True, vmem_limit_bytes=125 * 512 * 1024
        ),
    )(noise, data)
    if "nofin" in opts:
        return sums
    return pl.pallas_call(
        finish,
        out_shape=tuple(jax.ShapeDtypeStruct(v.shape, v.dtype) for v in sums),
        in_specs=[pl.BlockSpec(memory_space=pltpu.VMEM)] * 2,
        out_specs=[pl.BlockSpec(memory_space=pl.ANY)] * 2,
        scratch_shapes=[dma((2,))],
        compiler_params=pltpu.CompilerParams(vmem_limit_bytes=8 * 1024 * 1024),
    )(*sums)


def solution(mesh, stage=3, opts=()):
    return jax.shard_map(
        functools.partial(local, stage=stage, opts=opts),
        mesh=mesh,
        in_specs=(P("row", "col"), P("col", "row")),
        out_specs=(P(("row", "col"), None), P("col", "row")),
        check_vma=False,
    )
```
